32 devices in a mesh: row: 2 (over x), col: 4 (over y, core), head: 4 (over z).
Axes of the slice: x: 2, y: 2, z: 4, core: 2. Of those that a mesh axis runs over, the one named last changes fastest.
Arguments:
- tokens: bfloat16 [32, 128, 1024], P(('row', 'head'), 'col'), may hold values from -6 to 6
- valid: int32 [32, 128], P('row', 'col'), may hold values 0 or 1
- gain: float32 [1024], replicated, may hold values from 0.1 to 1.9
- w_qkv: bfloat16 [1024, 3, 1024], P(None, None, 'head'), may hold values from -0.1875 to 0.1875
- w_proj: bfloat16 [1024, 1024], P('head'), may hold values from -0.1875 to 0.1875
- rel_table: float32 [225, 16], P(None, 'head'), may hold values from -4 to 300
- cotangent: bfloat16 [32, 128, 1024], P(('row', 'head'), 'col'), may hold values from -6 to 6
Outputs:
- mixed: bfloat16 [32, 128, 1024], P(('row', 'head'), 'col')
- token_gradient: bfloat16 [32, 128, 1024], P(('row', 'head'), 'col')
- proj_grad: float32 [1024, 1024], P('head', ('row', 'col'))
- table_grad: float32 [225, 16], P(None, 'head')
The draws below stay inside these ranges and needn't reach their ends.
All inputs are finite; a program needn't handle non-finite values. No bound on the sum of `valid` on one device may be relied on, other than what follows from the above.
Results may differ from the reference program's by a relative error of at most 0.0078.
Values may be sent and summed in bfloat16 or wider, within the bound.
A program may use at most 64 MiB of HBM per device.

```python
import math
import jax
import jax.numpy as jnp
from jax import lax

D = 1024
HEADS = 16
HD = 64
WIN = 8
SHIFT = 4
H = 32
W = 128
N_HEAD = 4


def draw_rel_table(key, part):
    first = jax.random.fold_in(key, 0)
    count = (2 * WIN - 1) * (2 * WIN - 1)
    return jnp.clip(jax.random.normal(first, (count, HEADS), jnp.float32), -4.0, 4.0)


def place_ends(result, stream_key, least, top_value):
    dims = result.shape
    spot = [jax.random.randint(jax.random.fold_in(stream_key, axis), (), 0, dims[axis]) for axis in range(len(dims))]
    result = result.at[tuple(spot)].set(least)
    longest = dims.index(max(dims))
    spot[longest] = (spot[longest] + 1) % dims[longest]
    return result.at[tuple(spot)].set(top_value)


def strengthened(drawn, rng, source, target, parts, factor):
    def block_of(dim):
        return (jnp.arange(drawn.shape[dim]) // (drawn.shape[dim] // parts)).reshape((-1,) + (1,) * (drawn.ndim - 1 - dim))

    one_side = jax.random.permutation(rng, parts)[block_of(target)]
    far = (block_of(target) + parts // 2) % parts
    return jnp.where((block_of(source) == one_side) | (block_of(source) == far), factor * drawn, drawn)


def steps_of(rng, extent, cuts, smallest, largest):
    level = 1.0
    for axis_at, parts in cuts:
        draws = jax.random.uniform(jax.random.fold_in(jax.random.fold_in(rng, 6), axis_at), (parts,), jnp.float32, smallest / len(cuts), largest / len(cuts))
        level = level * jnp.repeat(jnp.exp(draws), extent[axis_at] // parts).reshape((-1,) + (1,) * (len(extent) - 1 - axis_at))
    return level


def scatter_about(stream_key, extent, deviation, most, pieces=(), kind=jnp.bfloat16):
    array = jax.random.normal(stream_key, extent, jnp.float32) * deviation
    if len(pieces) > 0:
        array = steps_of(stream_key, extent, pieces, -0.22, 0.18) * array
    return jnp.clip(array, min=-most, max=most).astype(kind)


def noise_with(stream_key, dims, deviation, bound, pieces, heavy, held_as=jnp.bfloat16):
    values = deviation * jax.random.normal(stream_key, dims, jnp.float32)
    if pieces:
        values = values * steps_of(stream_key, dims, pieces, -0.22, 0.18)
    return jnp.clip(strengthened(values, jax.random.fold_in(stream_key, 3), *heavy), -bound, bound).astype(held_as)


def setup_inputs(seed: int = 0) -> dict:
    streams_of = jax.random.split(jax.random.key(seed), 8)
    return {
        "tokens": scatter_about(streams_of[0], (H, W, D), 1.0, 6.0, ((0, 8), (1, 4))),
        "valid": place_ends((jax.random.randint(streams_of[1], (H, W), 0, 4) < 3).astype(jnp.int32), jax.random.fold_in(streams_of[1], 1), 0, 1),
        "gain": jnp.clip(1.0 + 0.18 * jax.random.normal(streams_of[2], (D,), jnp.float32), 0.1, 1.9),
        "w_qkv": scatter_about(streams_of[3], (D, 3, D), D ** -0.5, 0.1875, ((2, 4),)),
        "w_proj": scatter_about(streams_of[4], (D, D), D ** -0.5, 0.1875, ((0, 4),)),
        "rel_table": draw_rel_table(jax.random.fold_in(streams_of[7], 71), 0),
        "cotangent": noise_with(streams_of[6], (H, W, D), 1.0, 6.0, ((0, 8), (1, 4)), (0, 2, 8, 2.0)),
    }


EPS = 1e-05
HIGH = lax.Precision.HIGHEST

def region(index, grand_total):
    return jnp.where(index < grand_total - WIN, 0, jnp.where(index < grand_total - SHIFT, 1, 2)).astype(jnp.int32)

def offsets():
    span = 2 * WIN - 1
    pos = jnp.arange(WIN * WIN, dtype=jnp.int32)
    prow = pos // WIN
    pcol = pos % WIN
    index = (prow[:, None] - prow[None, :] + WIN - 1) * span + (pcol[:, None] - pcol[None, :] + WIN - 1)
    table_ids = jnp.arange(span * span, dtype=jnp.int32)
    return (index[:, :, None] == table_ids[None, None, :]).astype(jnp.float32).reshape(WIN * WIN * WIN * WIN, span * span)

def to_windows(block):
    nrow, ncol, heads, depth = block.shape
    block = block.reshape(nrow // WIN, WIN, ncol // WIN, WIN, heads, depth).transpose(0, 2, 4, 1, 3, 5)
    return block.reshape(nrow // WIN * (ncol // WIN), heads, WIN * WIN, depth)

def from_windows(block, nrow, ncol):
    count, heads, posn, depth = block.shape
    block = block.reshape(nrow // WIN, ncol // WIN, heads, WIN, WIN, depth).transpose(0, 3, 1, 4, 2, 5)
    return block.reshape(nrow, ncol, heads * depth)

def attend(qkv, grad, labels, valid, bias, onehot):
    nrow, ncol = labels.shape
    feature_width = qkv.shape[3]
    heads = feature_width // HD
    scale = HD ** (-0.5)
    query = to_windows(qkv[:, :, 0].reshape(nrow, ncol, heads, HD)).astype(jnp.float32)
    key = to_windows(qkv[:, :, 1].reshape(nrow, ncol, heads, HD)).astype(jnp.float32)
    value = to_windows(qkv[:, :, 2].reshape(nrow, ncol, heads, HD)).astype(jnp.float32)
    dout = to_windows(grad.reshape(nrow, ncol, heads, HD)).astype(jnp.float32)
    lab_win = to_windows(labels[:, :, None, None])[:, 0, :, 0]
    val_win = to_windows(valid[:, :, None, None])[:, 0, :, 0]
    diagonal = jnp.eye(WIN * WIN, dtype=bool)
    allowed = (lab_win[:, :, None] == lab_win[:, None, :]) & ((val_win[:, None, :] == 1) | diagonal[None])
    scores = jnp.einsum('wiqd,wikd->wiqk', query, key) * scale + bias[None]
    scores = jnp.where(allowed[:, None], scores, -1e+30)
    top = lax.optimization_barrier(jnp.max(scores, -1, keepdims=True))
    expo = jnp.exp(scores - top)
    prob = expo / lax.optimization_barrier(jnp.sum(expo, -1, keepdims=True))
    prob_b = prob.astype(jnp.bfloat16).astype(jnp.float32)
    attended = jnp.einsum('wiqk,wikd->wiqd', prob_b, value).astype(jnp.bfloat16)
    dprob = jnp.einsum('wiqd,wikd->wiqk', dout, value)
    dvalue = jnp.einsum('wiqk,wiqd->wikd', prob_b, dout).astype(jnp.bfloat16)
    dscore = prob * (dprob - lax.optimization_barrier(jnp.sum(prob * dprob, -1, keepdims=True)))
    dscore_b = dscore.astype(jnp.bfloat16).astype(jnp.float32)
    dquery = (jnp.einsum('wiqk,wikd->wiqd', dscore_b, key) * scale).astype(jnp.bfloat16)
    dkey = (jnp.einsum('wiqk,wiqd->wikd', dscore_b, query) * scale).astype(jnp.bfloat16)
    summed = lax.optimization_barrier(jnp.sum(dscore, 0)).transpose(1, 2, 0).reshape(WIN * WIN * WIN * WIN, heads)
    tgrad = jnp.dot(onehot.T, summed, precision=HIGH)
    grads = jnp.stack([from_windows(dquery, nrow, ncol), from_windows(dkey, nrow, ncol), from_windows(dvalue, nrow, ncol)], 2)
    return (from_windows(attended, nrow, ncol), grads, tgrad)

def reference(tokens, valid, gain, w_qkv, w_proj, rel_table, cotangent):
    nrow, ncol, feature_width = tokens.shape
    grand_total = nrow * ncol
    flat = tokens.reshape(grand_total, feature_width).astype(jnp.float32)
    token_average = lax.optimization_barrier(jnp.mean(flat, -1, keepdims=True))
    centered_input = flat - token_average
    inverse_deviation = lax.rsqrt(lax.optimization_barrier(jnp.mean(centered_input * centered_input, -1, keepdims=True)) + EPS)
    standardized_input = centered_input * inverse_deviation
    normalized_tokens = (standardized_input * gain).astype(jnp.bfloat16)
    qkv = jnp.dot(normalized_tokens, w_qkv.reshape(feature_width, 3 * feature_width), preferred_element_type=jnp.float32)
    qkv = qkv.astype(jnp.bfloat16).reshape(nrow, ncol, 3, feature_width)
    rolled = jnp.roll(qkv, (-SHIFT, -SHIFT), (0, 1))
    out_grad = jnp.dot(cotangent.reshape(grand_total, feature_width), w_proj.T, preferred_element_type=jnp.float32)
    out_grad = out_grad.astype(jnp.bfloat16).reshape(nrow, ncol, feature_width)
    rolled_grad = jnp.roll(out_grad, (-SHIFT, -SHIFT), (0, 1))
    onehot = offsets()
    bias = jnp.dot(onehot, rel_table, precision=HIGH).reshape(WIN * WIN, WIN * WIN, HEADS).transpose(2, 0, 1)
    col_lab = region(jnp.arange(ncol, dtype=jnp.int32), ncol)

    def band(index):
        start = index * WIN
        qkv_band = lax.dynamic_slice_in_dim(rolled, start, WIN, 0)
        grad_band = lax.dynamic_slice_in_dim(rolled_grad, start, WIN, 0)
        valid_band = lax.dynamic_slice_in_dim(valid, start, WIN, 0)
        row_lab = region(start + jnp.arange(WIN, dtype=jnp.int32), nrow)
        labels = 3 * row_lab[:, None] + col_lab[None, :]
        return attend(qkv_band, grad_band, labels, valid_band, bias, onehot)
    attended, grads, tparts = lax.map(band, jnp.arange(nrow // WIN, dtype=jnp.int32))
    attended = attended.reshape(nrow, ncol, feature_width)
    grads = grads.reshape(nrow, ncol, 3, feature_width)
    attn_out = jnp.roll(attended, (SHIFT, SHIFT), (0, 1)).reshape(grand_total, feature_width)
    qkv_grad = jnp.roll(grads, (SHIFT, SHIFT), (0, 1))
    group = feature_width // N_HEAD
    branch = jnp.zeros((grand_total, feature_width), jnp.float32)
    norm_grad = jnp.zeros((grand_total, feature_width), jnp.float32)
    for index in range(N_HEAD):
        low = index * group
        part = jnp.dot(attn_out[:, low:low + group], w_proj[low:low + group], preferred_element_type=jnp.float32)
        branch = branch + lax.optimization_barrier(part.astype(jnp.bfloat16)).astype(jnp.float32)
        piece = qkv_grad[:, :, :, low:low + group].reshape(grand_total, 3 * group)
        weights = w_qkv[:, :, low:low + group].reshape(feature_width, 3 * group)
        back = jnp.dot(piece, weights.T, preferred_element_type=jnp.float32)
        norm_grad = norm_grad + lax.optimization_barrier(back.astype(jnp.bfloat16)).astype(jnp.float32)
    mixed = (flat + branch).astype(jnp.bfloat16).reshape(nrow, ncol, feature_width)
    scale = 1.0 / math.sqrt(grand_total)
    proj_grad = jnp.dot(attn_out.T, cotangent.reshape(grand_total, feature_width), preferred_element_type=jnp.float32) * scale
    table_grad = lax.optimization_barrier(jnp.sum(tparts, 0)) * (WIN * scale)
    scaled_tokens = norm_grad * gain
    token_gradient = cotangent.reshape(grand_total, feature_width).astype(jnp.float32) + inverse_deviation * (scaled_tokens - lax.optimization_barrier(jnp.mean(scaled_tokens, -1, keepdims=True)) - standardized_input * lax.optimization_barrier(jnp.mean(scaled_tokens * standardized_input, -1, keepdims=True)))
    token_gradient = token_gradient.astype(jnp.bfloat16).reshape(nrow, ncol, feature_width)
    return (mixed, token_gradient, proj_grad, table_grad)
```

```python
import functools
import math

import jax
import jax.numpy as jnp
from jax import lax
from jax.experimental import pallas as pl
from jax.experimental.pallas import tpu as pltpu
from jax.sharding import PartitionSpec as P

HD = 64
WIN = 8
SHIFT = 4
UNIT = SHIFT * SHIFT
EPS = 1e-05
HIGH = lax.Precision.HIGHEST
MESH = pl.DeviceIdType.MESH
F32 = jnp.float32
BF16 = jnp.bfloat16
NN = (((1,), (0,)), ((), ()))
NT = (((1,), (1,)), ((), ()))
TN = (((0,), (0,)), ((), ()))


def dot(a, b, dims):
    return lax.dot_general(a, b, dims, preferred_element_type=F32)


def region(index, grand_total):
    return jnp.where(
        index < grand_total - WIN, 0, jnp.where(index < grand_total - SHIFT, 1, 2)
    ).astype(jnp.int32)


def window_places():
    pos = jnp.arange(WIN * WIN, dtype=jnp.int32)
    prow = pos // 32 * SHIFT + pos // SHIFT % SHIFT
    pcol = pos // 16 % 2 * SHIFT + pos % SHIFT
    return prow, pcol


def offsets():
    span = 2 * WIN - 1
    prow, pcol = window_places()
    index = (prow[:, None] - prow[None, :] + WIN - 1) * span + (
        pcol[:, None] - pcol[None, :] + WIN - 1
    )
    table_ids = jnp.arange(span * span, dtype=jnp.int32)
    return (
        (index[:, :, None] == table_ids[None, None, :])
        .astype(F32)
        .reshape(WIN * WIN * WIN * WIN, span * span)
    )


def to_units(block):
    nrow, ncol, width = block.shape
    block = block.reshape(nrow, ncol // SHIFT, SHIFT, width).transpose(1, 0, 2, 3)
    return block.reshape(nrow * ncol, width)


def from_units(block, nrow, ncol):
    width = block.shape[-1]
    block = block.reshape(ncol // SHIFT, nrow, SHIFT, width).transpose(1, 0, 2, 3)
    return block.reshape(nrow, ncol, width)


def kernel(
    sizes,
    tok_ref, cot_ref, gain_ref, wq_ref, wp_ref, bias_ref, mask_ref,
    mixed_ref, tg_ref, pg_ref, ts_ref,
    xhat, rstd, gath, tile, back, terms, recv, wsend, wrecv, tsend, trecv, tsum,
    ag_send, ag_recv, in_send, in_recv, out_send, out_recv, rs_send, rs_recv,
    pl_send, pl_recv,
):
    n, nr, nc, plane, direct = sizes
    h = lax.axis_index("head")
    r = lax.axis_index("row")
    c = lax.axis_index("col")
    part, width = tok_ref.shape
    group = wp_ref.shape[0]
    ucols = part // UNIT

    def at(dr, dc):
        return {"row": lax.rem(r + dr % nr, nr), "col": lax.rem(c + dc % nc, nc)}

    barrier = pltpu.get_barrier_semaphore()
    for dr, dc in plane:
        pl.semaphore_signal(barrier, inc=1, device_id=at(dr, dc), device_id_type=MESH)

    for dh in (1, n - 1):
        pl.semaphore_signal(
            barrier, inc=1, device_id={"head": lax.rem(h + dh, n)}, device_id_type=MESH
        )
    gath[0, h] = cot_ref[...]
    pl.semaphore_wait(barrier, len(plane) + 2)

    def ag_copy(arr, way, t, blk):
        step = 1 - 2 * way
        return pltpu.make_async_remote_copy(
            src_ref=gath.at[arr, blk], dst_ref=gath.at[arr, blk],
            send_sem=ag_send.at[arr, way, t], recv_sem=ag_recv.at[arr, way, t],
            device_id={"head": h + step}, device_id_type=MESH,
        )

    def sends(way, t):
        if way == 0:
            return (h < n - 1) & (h >= t)
        return (h > 0) & (h < n - t)

    def receives(way, t):
        return h > t if way == 0 else h < n - 1 - t

    def ag_send_step(arr, way, t):
        @pl.when(sends(way, t))
        def _():
            ag_copy(arr, way, t, h - (1 - 2 * way) * t).start()

    for way in range(2):
        ag_send_step(0, way, 0)

    x = tok_ref[...].astype(F32)
    cen = x - jnp.mean(x, -1, keepdims=True)
    inv = lax.rsqrt(jnp.mean(cen * cen, -1, keepdims=True) + EPS)
    std = cen * inv
    xhat[...] = std
    rstd[...] = inv
    gath[1, h] = (std * gain_ref[...]).astype(BF16)
    for way in range(2):
        ag_send_step(1, way, 0)

    def in_copy(k):
        if k == 0:
            src, dst, dev = tile.at[0, pl.ds(1, ucols - 1)], tile.at[n, pl.ds(1, ucols - 1)], at(-1, 0)
        elif k == n:
            src, dst, dev = tile.at[0, 0], tile.at[n, ucols], at(-1, -1)
        else:
            src, dst, dev = tile.at[k, 0], tile.at[k, ucols], at(0, -1)
        return pltpu.make_async_remote_copy(
            src_ref=src, dst_ref=dst, send_sem=in_send.at[k], recv_sem=in_recv.at[k],
            device_id=dev, device_id_type=MESH,
        )

    def project(blk):
        g = dot(gath[0, blk], wp_ref[...], NT).astype(BF16)
        q = dot(gath[1, blk], wq_ref[...], NN).astype(BF16)
        tile[blk, pl.ds(0, ucols), :, pl.ds(0, 3 * group)] = q.reshape(ucols, UNIT, 3 * group)
        tile[blk, pl.ds(0, ucols), :, pl.ds(3 * group, group)] = g.reshape(ucols, UNIT, group)
        for k in range(n):
            @pl.when(blk == k)
            def _():
                in_copy(k).start()
                if k == 0:
                    in_copy(n).start()

    project(h)
    for t in range(n - 1):
        for arr in range(2):
            for way in range(2):
                @pl.when(receives(way, t))
                def _():
                    step = 1 - 2 * way
                    pltpu.make_async_remote_copy(
                        src_ref=gath.at[arr, h - step * (t + 1)],
                        dst_ref=gath.at[arr, h - step * (t + 1)],
                        send_sem=ag_send.at[arr, way, t], recv_sem=ag_recv.at[arr, way, t],
                        device_id={"head": h - step}, device_id_type=MESH,
                    ).wait_recv()
                if t + 1 < n - 1:
                    ag_send_step(arr, way, t + 1)
        for way in range(2):
            @pl.when(receives(way, t))
            def _():
                project(h - (1 - 2 * way) * (t + 1))
    for k in range(n + 1):
        in_copy(k).wait_recv()

    lane = lax.broadcasted_iota(jnp.int32, (2 * WIN * WIN, 2 * HD), 1)
    first = lane < HD
    keep0 = jnp.where(first, 1.0, 0.0).astype(BF16)
    keep1 = jnp.where(first, 0.0, 1.0).astype(BF16)
    half = 2 * WIN * WIN
    scale = HD ** (-0.5)
    tsum[...] = jnp.zeros_like(tsum)

    def pair_step(i, jp):
        def places():
            return [(2 * i + 1 + ur, 4 * jp + 1 + 2 * w) for w in range(2) for ur in range(2)]

        def load(at_lane):
            return jnp.concatenate(
                [tile[ur, pl.ds(uc, 2), :, pl.ds(at_lane, 2 * HD)].reshape(2 * UNIT, 2 * HD) for ur, uc in places()], 0
            )

        def save(value, at_lane):
            for k, (ur, uc) in enumerate(places()):
                back[ur, pl.ds(uc, 2), :, pl.ds(at_lane, 2 * HD)] = (
                    value[2 * UNIT * k : 2 * UNIT * (k + 1)].astype(BF16).reshape(2, UNIT, 2 * HD)
                )

        for hp in range(group // (2 * HD)):
            base = hp * 2 * HD
            q, k, v, do = [load(base + s * group) for s in range(4)]
            qs = jnp.concatenate([q * keep0, q * keep1], 0)
            dos = jnp.concatenate([do * keep0, do * keep1], 0)
            m = mask_ref[2 * i + jp]
            s = dot(qs, k, NT) * scale + bias_ref[hp] + jnp.concatenate([m, m], 0)
            e = jnp.exp(s - jnp.max(s, -1, keepdims=True))
            p = e / jnp.sum(e, -1, keepdims=True)
            pb = p.astype(BF16)
            att = dot(pb, v, NN)
            save(jnp.where(first, att[:half], att[half:]), base)
            dp = dot(dos, v, NT)
            save(dot(pb, dos, TN), base + 3 * group)
            ds = p * (dp - jnp.sum(p * dp, -1, keepdims=True))
            dsb = ds.astype(BF16)
            dq = dot(dsb, k, NN) * scale
            save(jnp.where(first, dq[:half], dq[half:]), base + group)
            save(dot(dsb, qs, TN) * scale, base + 2 * group)
            tsum[hp] += ds

    def out_copy(k):
        if k == 0:
            src, dst, dev = back.at[n, pl.ds(1, ucols - 1)], back.at[0, pl.ds(1, ucols - 1)], at(1, 0)
        elif k == 1:
            src, dst, dev = back.at[n, ucols], back.at[0, 0], at(1, 1)
        else:
            src, dst, dev = back.at[k - 1, ucols], back.at[k - 1, 0], at(0, 1)
        return pltpu.make_async_remote_copy(
            src_ref=src, dst_ref=dst, send_sem=out_send.at[k], recv_sem=out_recv.at[k],
            device_id=dev, device_id_type=MESH,
        )

    for i in range(n // 2 - 1, -1, -1):
        for jp in range(ucols // 4):
            pair_step(i, jp)
        if i == n // 2 - 1:
            out_copy(0).start()
            out_copy(1).start()
    for k in range(1, n):
        out_copy(k + 1).start()

    low = lax.broadcasted_iota(jnp.int32, (WIN * WIN, 2 * HD), 1) < HD
    for hp in range(group // (2 * HD)):
        folds = []
        for k in range(2):
            f = tsum[hp, k * half : k * half + HD] + tsum[hp, k * half + HD : (k + 1) * half]
            folds.append(f + pltpu.roll(f, HD, 1))
        tsend[hp] = jnp.where(low, folds[0], folds[1])

    for k in range(n + 1):
        out_copy(k).wait_recv()

    def block(d, start, count):
        return back[d, pl.ds(0, ucols), :, pl.ds(start, count)].reshape(part, count)

    def rs_copy(arr, way, d):
        step = 1 - 2 * way
        return pltpu.make_async_remote_copy(
            src_ref=terms.at[arr, d], dst_ref=recv.at[arr, way, d],
            send_sem=rs_send.at[arr, way, d], recv_sem=rs_recv.at[arr, way, d],
            device_id={"head": h + step}, device_id_type=MESH,
        )

    def rs_arrived(arr, way, d):
        step = 1 - 2 * way
        pltpu.make_async_remote_copy(
            src_ref=terms.at[arr, d], dst_ref=recv.at[arr, way, d],
            send_sem=rs_send.at[arr, way, d], recv_sem=rs_recv.at[arr, way, d],
            device_id={"head": h - step}, device_id_type=MESH,
        ).wait_recv()

    order = []
    for k in range(n // 2):
        order += [n - 1 - k, k]
    for arr in range(2):
        for d in order:
            if arr == 0:
                term = dot(block(d, 0, group), wp_ref[...], NN)
            else:
                term = dot(block(d, group, 3 * group), wq_ref[...], NT)
            terms[arr, d] = term.astype(BF16)
            if d > 0:
                @pl.when(h == 0)
                def _():
                    rs_copy(arr, 0, d).start()
            if d < n - 1:
                @pl.when(h == n - 1)
                def _():
                    rs_copy(arr, 1, d).start()

    def pl_copy(kind, o):
        dr, dc = plane[o]
        there = at(dr, dc)
        if kind == 0:
            src, dst = wsend.at[there["row"] * nc + there["col"]], wrecv.at[o]
        else:
            src, dst = tsend, trecv.at[o]
        return pltpu.make_async_remote_copy(
            src_ref=src, dst_ref=dst, send_sem=pl_send.at[kind, o], recv_sem=pl_recv.at[kind, o],
            device_id=there, device_id_type=MESH,
        )

    attn = jnp.concatenate([block(d, 0, group) for d in range(n)], 0)
    grad = gath[0].reshape(n * part, width)
    wterm = dot(attn, grad, TN)
    if direct:
        piece = width // (nr * nc)
        for j in range(nr * nc):
            wsend[j] = wterm[:, j * piece : (j + 1) * piece].astype(BF16)
        for o in range(len(plane)):
            for kind in range(2):
                pl_copy(kind, o).start()
    else:
        pg_ref[...] = wterm
        ts_ref[...] = tsend[...]

    for arr in range(2):
        for d in order:
            if d > 1:
                @pl.when((h > 0) & (h < d))
                def _():
                    rs_arrived(arr, 0, d)
                    terms[arr, d] = (terms[arr, d].astype(F32) + recv[arr, 0, d].astype(F32)).astype(BF16)
                    rs_copy(arr, 0, d).start()
            if d < n - 2:
                @pl.when((h > d) & (h < n - 1))
                def _():
                    rs_arrived(arr, 1, d)
                    terms[arr, d] = (terms[arr, d].astype(F32) + recv[arr, 1, d].astype(F32)).astype(BF16)
                    rs_copy(arr, 1, d).start()

    def total(arr):
        xhat2 = terms.at[arr, h]
        sides = [h > 0, h < n - 1]
        for way in range(2):
            @pl.when(sides[way])
            def _():
                rs_arrived(arr, way, h)

            @pl.when(jnp.logical_not(sides[way]))
            def _():
                recv[arr, way, h] = jnp.zeros((part, width), BF16)
        return xhat2[...].astype(F32) + recv[arr, 0, h].astype(F32) + recv[arr, 1, h].astype(F32)

    mixed_ref[...] = (tok_ref[...].astype(F32) + total(0)).astype(BF16)
    gg = total(1) * gain_ref[...]
    std = xhat[...]
    tg_ref[...] = (
        cot_ref[...].astype(F32)
        + rstd[...]
        * (
            gg
            - jnp.mean(gg, -1, keepdims=True)
            - std * jnp.mean(gg * std, -1, keepdims=True)
        )
    ).astype(BF16)

    if direct:
        for o in range(len(plane)):
            for kind in range(2):
                pl_copy(kind, o).wait_recv()
        wsum = wsend[r * nc + c].astype(F32)
        tall = tsend[...]
        for o in range(len(plane)):
            wsum = wsum + wrecv[o].astype(F32)
            tall = tall + trecv[o]
        pg_ref[...] = wsum
        ts_ref[...] = tall
        for o in range(len(plane)):
            for kind in range(2):
                pl_copy(kind, o).wait_send()

    for arr in range(2):
        for way in range(2):
            for t in range(n - 1):
                @pl.when(sends(way, t))
                def _():
                    ag_copy(arr, way, t, h - (1 - 2 * way) * t).wait_send()
    for k in range(n + 1):
        in_copy(k).wait_send()
        out_copy(k).wait_send()
    for arr in range(2):
        for d in range(n):
            if d > 0:
                @pl.when(h < d)
                def _():
                    rs_copy(arr, 0, d).wait_send()
            if d < n - 1:
                @pl.when(h > d)
                def _():
                    rs_copy(arr, 1, d).wait_send()


def on_device(n, nr, nc, tokens, valid, gain, w_qkv, w_proj, rel_table, cotangent):
    part_rows, ncol, width = tokens.shape
    tile_rows = part_rows * n
    part = part_rows * ncol
    heads = rel_table.shape[1]
    group = heads * HD
    pairs = heads // 2
    pos = WIN * WIN
    ucols = ncol // SHIFT

    row_lab = region(
        lax.axis_index("row") * tile_rows + jnp.arange(tile_rows, dtype=jnp.int32), tile_rows * nr
    )
    col_lab = region(lax.axis_index("col") * ncol + jnp.arange(ncol, dtype=jnp.int32), ncol * nc)
    labels = 3 * row_lab[:, None] + col_lab[None, :]

    def to_pairs(block):
        block = block.reshape(tile_rows // WIN, 2, SHIFT, ncol // WIN, 2, SHIFT)
        return block.transpose(0, 3, 1, 4, 2, 5).reshape(-1, 2 * pos)

    lab = to_pairs(labels) + 16 * (jnp.arange(2 * pos, dtype=jnp.int32) // pos)[None]
    val = to_pairs(valid)
    allowed = (lab[:, :, None] == lab[:, None, :]) & (
        (val[:, None, :] == 1) | jnp.eye(2 * pos, dtype=bool)[None]
    )
    mask = jnp.where(allowed, 0.0, -1e30).astype(F32)
    onehot = offsets()
    bias = jnp.dot(onehot, rel_table, precision=HIGH).reshape(pos, pos, heads).transpose(2, 0, 1)
    bias = jnp.broadcast_to(
        bias.reshape(pairs, 2, 1, pos, 1, pos), (pairs, 2, 2, pos, 2, pos)
    ).reshape(pairs, 4 * pos, 2 * pos)

    direct = nr * nc <= 8
    if direct:
        plane = [(dr, dc) for dr in range(nr) for dc in range(nc) if (dr, dc) != (0, 0)]
    else:
        six = [(1, 0), (nr - 1, 0), (0, 1), (0, nc - 1), (1, 1), (nr - 1, nc - 1)]
        plane = sorted(set(six))
    count = len(plane)
    piece = width // (nr * nc)
    vmem = pl.BlockSpec(memory_space=pltpu.VMEM)
    dma = pltpu.SemaphoreType.DMA
    mixed, token_gradient, wsum, tall = pl.pallas_call(
        functools.partial(kernel, (n, nr, nc, tuple(plane), direct)),
        out_shape=(
            jax.ShapeDtypeStruct((part, width), BF16),
            jax.ShapeDtypeStruct((part, width), BF16),
            jax.ShapeDtypeStruct((group, piece if direct else width), F32),
            jax.ShapeDtypeStruct((pairs, pos, 2 * HD), F32),
        ),
        in_specs=[vmem] * 7,
        out_specs=[vmem] * 4,
        scratch_shapes=[
            pltpu.VMEM((part, width), F32),
            pltpu.VMEM((part, 1), F32),
            pltpu.VMEM((2, n, part, width), BF16),
            pltpu.VMEM((n + 1, ucols + 1, UNIT, 4 * group), BF16),
            pltpu.VMEM((n + 1, ucols + 1, UNIT, 4 * group), BF16),
            pltpu.VMEM((2, n, part, width), BF16),
            pltpu.VMEM((2, 2, n, part, width), BF16),
            pltpu.VMEM((nr * nc, group, piece) if direct else (1, 16, 128), BF16),
            pltpu.VMEM((count, group, piece) if direct else (1, 16, 128), BF16),
            pltpu.VMEM((pairs, pos, 2 * HD), F32),
            pltpu.VMEM((count, pairs, pos, 2 * HD) if direct else (1, 16, 128), F32),
            pltpu.VMEM((pairs, 4 * pos, 2 * pos), F32),
            dma((2, 2, n)),
            dma((2, 2, n)),
            dma((n + 1,)),
            dma((n + 1,)),
            dma((n + 1,)),
            dma((n + 1,)),
            dma((2, 2, n)),
            dma((2, 2, n)),
            dma((2, count)),
            dma((2, count)),
        ],
        compiler_params=pltpu.CompilerParams(
            collective_id=0, has_side_effects=True, vmem_limit_bytes=48 * 1024 * 1024
        ),
    )(
        to_units(tokens),
        to_units(cotangent),
        gain[None],
        w_qkv.reshape(width, 3 * group),
        w_proj,
        bias,
        mask,
    )
    if not direct:
        wsum = lax.psum_scatter(wsum, ("row", "col"), scatter_dimension=1, tiled=True)
        tall = lax.psum(tall, ("row", "col"))
    scale = 1.0 / math.sqrt(tile_rows * ncol * nr * nc)
    summed = tall.reshape(pairs, pos, 2, pos).transpose(1, 3, 0, 2).reshape(pos * pos, heads)
    table_grad = jnp.dot(onehot.T, summed, precision=HIGH) * (WIN * scale)
    return (
        from_units(mixed, part_rows, ncol),
        from_units(token_gradient, part_rows, ncol),
        wsum * scale,
        table_grad,
    )


def solution(mesh):
    n, nr, nc = (mesh.shape[name] for name in ("head", "row", "col"))
    return jax.shard_map(
        functools.partial(on_device, n, nr, nc),
        mesh=mesh,
        in_specs=(
            P(("row", "head"), "col", None),
            P("row", "col"),
            P(),
            P(None, None, "head"),
            P("head", None),
            P(None, "head"),
            P(("row", "head"), "col", None),
        ),
        out_specs=(
            P(("row", "head"), "col", None),
            P(("row", "head"), "col", None),
            P("head", ("row", "col")),
            P(None, "head"),
        ),
        check_vma=False,
    )
```

```python
import functools
import math

import jax
import jax.numpy as jnp
from jax import lax
from jax.experimental import pallas as pl
from jax.experimental.pallas import tpu as pltpu
from jax.sharding import PartitionSpec as P

HD = 64
WIN = 8
SHIFT = 4
UNIT = SHIFT * SHIFT
EPS = 1e-05
HIGH = lax.Precision.HIGHEST
MESH = pl.DeviceIdType.MESH
F32 = jnp.float32
BF16 = jnp.bfloat16
NN = (((1,), (0,)), ((), ()))
NT = (((1,), (1,)), ((), ()))
TN = (((0,), (0,)), ((), ()))


def dot(a, b, dims):
    return lax.dot_general(a, b, dims, preferred_element_type=F32)


def region(index, grand_total):
    return jnp.where(
        index < grand_total - WIN, 0, jnp.where(index < grand_total - SHIFT, 1, 2)
    ).astype(jnp.int32)


def window_places():
    pos = jnp.arange(WIN * WIN, dtype=jnp.int32)
    prow = pos // 32 * SHIFT + pos // SHIFT % SHIFT
    pcol = pos // 16 % 2 * SHIFT + pos % SHIFT
    return prow, pcol


def offsets():
    span = 2 * WIN - 1
    prow, pcol = window_places()
    index = (prow[:, None] - prow[None, :] + WIN - 1) * span + (
        pcol[:, None] - pcol[None, :] + WIN - 1
    )
    table_ids = jnp.arange(span * span, dtype=jnp.int32)
    return (
        (index[:, :, None] == table_ids[None, None, :])
        .astype(F32)
        .reshape(WIN * WIN * WIN * WIN, span * span)
    )


def kernel(
    sizes,
    tok_ref, cot_ref, gain_ref, wq_ref, wp_ref, bias_ref, mask_ref,
    mixed_ref, tg_ref, pg_ref, ts_ref,
    xhat, rstd, gath, tile_q, tile_g, back_a, back_d, probs, terms, recv, wsend, wrecv, tsend, trecv, tsum,
    ag_send, ag_recv, in_send, in_recv, out_send, out_recv, rs_send, rs_recv,
    pl_send, pl_recv,
):
    n, nr, nc, plane, direct, ncol, pg_scale = sizes
    h = lax.axis_index("head")
    r = lax.axis_index("row")
    c = lax.axis_index("col")
    part, width = tok_ref.shape
    group = wp_ref.shape[0]
    ucols = part // UNIT
    COT, NORM = 0, 1

    def at(dr, dc):
        return {"row": lax.rem(r + dr % nr, nr), "col": lax.rem(c + dc % nc, nc)}

    barrier = pltpu.get_barrier_semaphore()
    for dr, dc in plane:
        pl.semaphore_signal(barrier, inc=1, device_id=at(dr, dc), device_id_type=MESH)
    for dh in (1, n - 1):
        pl.semaphore_signal(
            barrier, inc=1, device_id={"head": lax.rem(h + dh, n)}, device_id_type=MESH
        )

    unit_at = lax.broadcasted_iota(jnp.int32, (part, part), 0)
    patch_at = lax.broadcasted_iota(jnp.int32, (part, part), 1)
    wanted = unit_at // SHIFT % SHIFT * ncol + unit_at // UNIT * SHIFT + unit_at % SHIFT
    perm = jnp.where(wanted == patch_at, 1.0, 0.0).astype(BF16)

    x = dot(perm, tok_ref[...], NN)
    cen = x - jnp.mean(x, -1, keepdims=True)
    inv = lax.rsqrt(jnp.mean(cen * cen, -1, keepdims=True) + EPS)
    std = cen * inv
    xhat[...] = std
    rstd[...] = inv
    gath[NORM, h] = (std * gain_ref[...]).astype(BF16)
    gath[COT, h] = dot(perm, cot_ref[...], NN).astype(BF16)
    pl.semaphore_wait(barrier, len(plane) + 2)

    def ag_copy(arr, way, t, blk):
        step = 1 - 2 * way
        return pltpu.make_async_remote_copy(
            src_ref=gath.at[arr, blk], dst_ref=gath.at[arr, blk],
            send_sem=ag_send.at[arr, way, t], recv_sem=ag_recv.at[arr, way, t],
            device_id={"head": h + step}, device_id_type=MESH,
        )

    def sends(way, t):
        if way == 0:
            return (h < n - 1) & (h >= t)
        return (h > 0) & (h < n - t)

    def receives(way, t):
        return h > t if way == 0 else h < n - 1 - t

    def ag_send_step(arr, way, t):
        @pl.when(sends(way, t))
        def _():
            ag_copy(arr, way, t, h - (1 - 2 * way) * t).start()

    def ag_receive_step(arr, way, t):
        @pl.when(receives(way, t))
        def _():
            step = 1 - 2 * way
            pltpu.make_async_remote_copy(
                src_ref=gath.at[arr, h - step * (t + 1)],
                dst_ref=gath.at[arr, h - step * (t + 1)],
                send_sem=ag_send.at[arr, way, t], recv_sem=ag_recv.at[arr, way, t],
                device_id={"head": h - step}, device_id_type=MESH,
            ).wait_recv()
        if t + 1 < n - 1:
            ag_send_step(arr, way, t + 1)

    def cot_after(t):
        @pl.when((h == t) & (h < n - 1))
        def _():
            ag_copy(COT, 0, 0, h).start()

        @pl.when((h == n - 1 - t) & (h > 0))
        def _():
            ag_copy(COT, 1, 0, h).start()

    def in_copy(kind, k):
        tile = (tile_q, tile_g)[kind]
        if k == 0:
            src, dst, dev = tile.at[0, pl.ds(1, ucols - 1)], tile.at[n, pl.ds(1, ucols - 1)], at(-1, 0)
        elif k == n:
            src, dst, dev = tile.at[0, 0], tile.at[n, ucols], at(-1, -1)
        else:
            src, dst, dev = tile.at[k, 0], tile.at[k, ucols], at(0, -1)
        return pltpu.make_async_remote_copy(
            src_ref=src, dst_ref=dst, send_sem=in_send.at[kind, k], recv_sem=in_recv.at[kind, k],
            device_id=dev, device_id_type=MESH,
        )

    def project(kind, blk):
        if kind == 0:
            for s in range(3):
                out = dot(gath[NORM, blk], wq_ref[s], NN).astype(BF16)
                tile_q[blk, pl.ds(0, ucols), :, pl.ds(s * group, group)] = out.reshape(
                    ucols, UNIT, group
                )
        else:
            out = dot(gath[COT, blk], wp_ref[...], NT).astype(BF16)
            tile_g[blk, pl.ds(0, ucols)] = out.reshape(ucols, UNIT, group)
        for k in range(n):
            @pl.when(blk == k)
            def _():
                in_copy(kind, k).start()
                if k == 0:
                    in_copy(kind, n).start()

    def project_step(kind, t):
        for way in range(2):
            @pl.when(receives(way, t))
            def _():
                project(kind, h - (1 - 2 * way) * (t + 1))

    for way in range(2):
        ag_send_step(NORM, way, 0)
    cot_after(0)
    project(0, h)
    for t in range(n - 1):
        for way in range(2):
            ag_receive_step(NORM, way, t)
        cot_after(t + 1)
        project_step(0, t)
    project(1, h)
    for way in range(2):
        ag_receive_step(COT, way, 0)
    project_step(1, 0)
    for k in range(n + 1):
        in_copy(0, k).wait_recv()

    lane = lax.broadcasted_iota(jnp.int32, (2 * WIN * WIN, 2 * HD), 1)
    first = lane < HD
    keep0 = jnp.where(first, 1.0, 0.0).astype(BF16)
    keep1 = jnp.where(first, 0.0, 1.0).astype(BF16)
    half = 2 * WIN * WIN
    scale = HD ** (-0.5)
    heads2 = group // (2 * HD)
    pairs2 = ucols // 4

    def places(i, jp):
        return [(2 * i + 1 + ur, 4 * jp + 1 + 2 * w) for w in range(2) for ur in range(2)]

    def load(tile, i, jp, at_lane):
        return jnp.concatenate(
            [
                tile[ur, pl.ds(uc, 2), :, pl.ds(at_lane, 2 * HD)].reshape(2 * UNIT, 2 * HD)
                for ur, uc in places(i, jp)
            ],
            0,
        )

    def save(tile, i, jp, at_lane, value):
        for k, (ur, uc) in enumerate(places(i, jp)):
            tile[ur, pl.ds(uc, 2), :, pl.ds(at_lane, 2 * HD)] = (
                value[2 * UNIT * k : 2 * UNIT * (k + 1)].astype(BF16).reshape(2, UNIT, 2 * HD)
            )

    def both(value):
        return jnp.concatenate([value * keep0, value * keep1], 0)

    def chosen(value):
        return jnp.where(first, value[:half], value[half:])

    def forward(i, jp):
        for hp in range(heads2):
            base = hp * 2 * HD
            q, k, v = [load(tile_q, i, jp, base + s * group) for s in range(3)]
            m = mask_ref[pairs2 * i + jp]
            s = dot(both(q), k, NT) * scale + bias_ref[hp] + jnp.concatenate([m, m], 0)
            e = jnp.exp(s - jnp.max(s, -1, keepdims=True))
            p = e / jnp.sum(e, -1, keepdims=True)
            probs[pairs2 * i + jp, hp] = p
            save(back_a, i, jp, base, chosen(dot(p.astype(BF16), v, NN)))

    def backward(i, jp):
        for hp in range(heads2):
            base = hp * 2 * HD
            q, k, v = [load(tile_q, i, jp, base + s * group) for s in range(3)]
            dos = both(load(tile_g, i, jp, base))
            p = probs[pairs2 * i + jp, hp]
            dp = dot(dos, v, NT)
            save(back_d, i, jp, base + 2 * group, dot(p.astype(BF16), dos, TN))
            ds = p * (dp - jnp.sum(p * dp, -1, keepdims=True))
            dsb = ds.astype(BF16)
            save(back_d, i, jp, base, chosen(dot(dsb, k, NN) * scale))
            save(back_d, i, jp, base + group, dot(dsb, both(q), TN) * scale)
            tsum[hp] += ds

    def out_copy(kind, k):
        back = (back_a, back_d)[kind]
        if k == 0:
            src, dst, dev = back.at[n, pl.ds(1, ucols - 1)], back.at[0, pl.ds(1, ucols - 1)], at(1, 0)
        elif k == n:
            src, dst, dev = back.at[n, ucols], back.at[0, 0], at(1, 1)
        else:
            src, dst, dev = back.at[k, ucols], back.at[k, 0], at(0, 1)
        return pltpu.make_async_remote_copy(
            src_ref=src, dst_ref=dst, send_sem=out_send.at[kind, k], recv_sem=out_recv.at[kind, k],
            device_id=dev, device_id_type=MESH,
        )

    def windows(kind, step, between):
        for i in range(n // 2 - 1, -1, -1):
            for jp in range(pairs2 - 1, -1, -1):
                step(i, jp)
                if jp == pairs2 - 1:
                    for k in (2 * i + 1, 2 * i + 2):
                        out_copy(kind, k if k < n else n).start()
            if i == n // 2 - 1:
                out_copy(kind, 0).start()
            between(i)

    def between_forward(i):
        if i == n // 2 - 1:
            for t in range(1, n - 2):
                for way in range(2):
                    ag_receive_step(COT, way, t)

    windows(0, forward, between_forward)
    for t in range(1, n - 2):
        project_step(1, t)
    for k in range(n + 1):
        out_copy(0, k).wait_recv()

    def block(back, d):
        return back[d, pl.ds(0, ucols)].reshape(part, back.shape[-1])

    def rs_copy(arr, way, d):
        step = 1 - 2 * way
        return pltpu.make_async_remote_copy(
            src_ref=terms.at[arr, d], dst_ref=recv.at[arr, way, d],
            send_sem=rs_send.at[arr, way, d], recv_sem=rs_recv.at[arr, way, d],
            device_id={"head": h + step}, device_id_type=MESH,
        )

    def rs_arrived(arr, way, d):
        step = 1 - 2 * way
        pltpu.make_async_remote_copy(
            src_ref=terms.at[arr, d], dst_ref=recv.at[arr, way, d],
            send_sem=rs_send.at[arr, way, d], recv_sem=rs_recv.at[arr, way, d],
            device_id={"head": h - step}, device_id_type=MESH,
        ).wait_recv()

    order = []
    for k in range(n // 2):
        order += [n - 1 - k, k]

    def rs_start(arr):
        for d in order:
            if arr == 0:
                term = dot(block(back_a, d), wp_ref[...], NN)
            else:
                grads = block(back_d, d)
                term = sum(
                    dot(grads[:, s * group : (s + 1) * group], wq_ref[s], NT) for s in range(3)
                )
            terms[arr, d] = term.astype(BF16)
            if d > 0:
                @pl.when(h == 0)
                def _():
                    rs_copy(arr, 0, d).start()
            if d < n - 1:
                @pl.when(h == n - 1)
                def _():
                    rs_copy(arr, 1, d).start()

    def pass_on(arr, way, d):
        rs_arrived(arr, way, d)
        terms[arr, d] = (terms[arr, d].astype(F32) + recv[arr, way, d].astype(F32)).astype(BF16)
        rs_copy(arr, way, d).start()

    def rs_transit(arr, d):
        if d > 1:
            @pl.when((h > 0) & (h < d))
            def _():
                pass_on(arr, 0, d)
        if d < n - 2:
            @pl.when((h > d) & (h < n - 1))
            def _():
                pass_on(arr, 1, d)

    def total(arr):
        sides = [h > 0, h < n - 1]
        for way in range(2):
            @pl.when(sides[way])
            def _():
                rs_arrived(arr, way, h)

            @pl.when(jnp.logical_not(sides[way]))
            def _():
                recv[arr, way, h] = jnp.zeros((part, width), BF16)
        return (
            terms[arr, h].astype(F32) + recv[arr, 0, h].astype(F32) + recv[arr, 1, h].astype(F32)
        )

    rs_start(0)
    for way in range(2):
        ag_receive_step(COT, way, n - 2)
    project_step(1, n - 2)
    for k in range(n + 1):
        in_copy(1, k).wait_recv()

    def between_backward(i):
        for d in order[: n // 2] if i == n // 2 - 1 else order[n // 2 :]:
            rs_transit(0, d)

    tsum[...] = jnp.zeros_like(tsum)
    windows(1, backward, between_backward)

    low = lax.broadcasted_iota(jnp.int32, (WIN * WIN, 2 * HD), 1) < HD
    for hp in range(heads2):
        folds = []
        for k in range(2):
            f = tsum[hp, k * half : k * half + HD] + tsum[hp, k * half + HD : (k + 1) * half]
            folds.append(f + pltpu.roll(f, HD, 1))
        tsend[hp] = jnp.where(low, folds[0], folds[1])

    for k in range(n + 1):
        out_copy(1, k).wait_recv()
    rs_start(1)

    def pl_copy(kind, o):
        dr, dc = plane[o]
        there = at(dr, dc)
        if kind == 0:
            src, dst = wsend.at[there["row"] * nc + there["col"]], wrecv.at[o]
        else:
            src, dst = tsend, trecv.at[o]
        return pltpu.make_async_remote_copy(
            src_ref=src, dst_ref=dst, send_sem=pl_send.at[kind, o], recv_sem=pl_recv.at[kind, o],
            device_id=there, device_id_type=MESH,
        )

    attn = jnp.concatenate([block(back_a, d) for d in range(n)], 0)
    wterm = dot(attn, gath[COT].reshape(n * part, width), TN)
    if direct:
        piece = width // (nr * nc)
        for j in range(nr * nc):
            wsend[j] = wterm[:, j * piece : (j + 1) * piece].astype(BF16)
        for o in range(len(plane)):
            for kind in range(2):
                pl_copy(kind, o).start()
    else:
        pg_ref[...] = wterm
        ts_ref[...] = tsend[...]

    for d in order:
        rs_transit(1, d)

    mixed = dot(perm, tok_ref[...], NN) + total(0)
    mixed_ref[...] = dot(perm, mixed.astype(BF16), TN).astype(BF16)

    if direct:
        for o in range(len(plane)):
            for kind in range(2):
                pl_copy(kind, o).wait_recv()
        wsum = wsend[r * nc + c].astype(F32)
        tall = tsend[...]
        for o in range(len(plane)):
            wsum = wsum + wrecv[o].astype(F32)
            tall = tall + trecv[o]
        pg_ref[...] = wsum * pg_scale
        ts_ref[...] = tall
        for o in range(len(plane)):
            for kind in range(2):
                pl_copy(kind, o).wait_send()

    gg = total(1) * gain_ref[...]
    std = xhat[...]
    tg = gath[COT, h].astype(F32) + rstd[...] * (
        gg - jnp.mean(gg, -1, keepdims=True) - std * jnp.mean(gg * std, -1, keepdims=True)
    )
    tg_ref[...] = dot(perm, tg.astype(BF16), TN).astype(BF16)

    for arr in range(2):
        for way in range(2):
            for t in range(n - 1):
                @pl.when(sends(way, t))
                def _():
                    ag_copy(arr, way, t, h - (1 - 2 * way) * t).wait_send()
    for kind in range(2):
        for k in range(n + 1):
            in_copy(kind, k).wait_send()
            out_copy(kind, k).wait_send()
    for arr in range(2):
        for d in range(n):
            if d > 0:
                @pl.when(h < d)
                def _():
                    rs_copy(arr, 0, d).wait_send()
            if d < n - 1:
                @pl.when(h > d)
                def _():
                    rs_copy(arr, 1, d).wait_send()


def on_device(n, nr, nc, tokens, valid, gain, w_qkv, w_proj, rel_table, cotangent):
    part_rows, ncol, width = tokens.shape
    tile_rows = part_rows * n
    part = part_rows * ncol
    heads = rel_table.shape[1]
    group = heads * HD
    pairs = heads // 2
    pos = WIN * WIN
    ucols = ncol // SHIFT

    row_lab = region(
        lax.axis_index("row") * tile_rows + jnp.arange(tile_rows, dtype=jnp.int32), tile_rows * nr
    )
    col_lab = region(lax.axis_index("col") * ncol + jnp.arange(ncol, dtype=jnp.int32), ncol * nc)
    labels = 3 * row_lab[:, None] + col_lab[None, :]

    def to_pairs(block):
        block = block.reshape(tile_rows // WIN, 2, SHIFT, ncol // WIN, 2, SHIFT)
        return block.transpose(0, 3, 1, 4, 2, 5).reshape(-1, 2 * pos)

    lab = to_pairs(labels) + 16 * (jnp.arange(2 * pos, dtype=jnp.int32) // pos)[None]
    val = to_pairs(valid)
    allowed = (lab[:, :, None] == lab[:, None, :]) & (
        (val[:, None, :] == 1) | jnp.eye(2 * pos, dtype=bool)[None]
    )
    mask = jnp.where(allowed, 0.0, -1e30).astype(F32)
    onehot = offsets()
    bias = jnp.dot(onehot, rel_table, precision=HIGH).reshape(pos, pos, heads).transpose(2, 0, 1)
    bias = jnp.broadcast_to(
        bias.reshape(pairs, 2, 1, pos, 1, pos), (pairs, 2, 2, pos, 2, pos)
    ).reshape(pairs, 4 * pos, 2 * pos)

    scale = 1.0 / math.sqrt(tile_rows * ncol * nr * nc)
    direct = nr * nc <= 8
    if direct:
        plane = [(dr, dc) for dr in range(nr) for dc in range(nc) if (dr, dc) != (0, 0)]
    else:
        six = [(1, 0), (nr - 1, 0), (0, 1), (0, nc - 1), (1, 1), (nr - 1, nc - 1)]
        plane = sorted(set(six))
    count = len(plane)
    piece = width // (nr * nc)
    vmem = pl.BlockSpec(memory_space=pltpu.VMEM)
    dma = pltpu.SemaphoreType.DMA
    mixed, token_gradient, wsum, tall = pl.pallas_call(
        functools.partial(kernel, (n, nr, nc, tuple(plane), direct, ncol, scale)),
        out_shape=(
            jax.ShapeDtypeStruct((part, width), BF16),
            jax.ShapeDtypeStruct((part, width), BF16),
            jax.ShapeDtypeStruct((group, piece if direct else width), F32),
            jax.ShapeDtypeStruct((pairs, pos, 2 * HD), F32),
        ),
        in_specs=[vmem] * 7,
        out_specs=[vmem] * 4,
        scratch_shapes=[
            pltpu.VMEM((part, width), F32),
            pltpu.VMEM((part, 1), F32),
            pltpu.VMEM((2, n, part, width), BF16),
            pltpu.VMEM((n + 1, ucols + 1, UNIT, 3 * group), BF16),
            pltpu.VMEM((n + 1, ucols + 1, UNIT, group), BF16),
            pltpu.VMEM((n + 1, ucols + 1, UNIT, group), BF16),
            pltpu.VMEM((n + 1, ucols + 1, UNIT, 3 * group), BF16),
            pltpu.VMEM((n * ucols // 8, pairs, 4 * pos, 2 * pos), F32),
            pltpu.VMEM((2, n, part, width), BF16),
            pltpu.VMEM((2, 2, n, part, width), BF16),
            pltpu.VMEM((nr * nc, group, piece) if direct else (1, 16, 128), BF16),
            pltpu.VMEM((count, group, piece) if direct else (1, 16, 128), BF16),
            pltpu.VMEM((pairs, pos, 2 * HD), F32),
            pltpu.VMEM((count, pairs, pos, 2 * HD) if direct else (1, 16, 128), F32),
            pltpu.VMEM((pairs, 4 * pos, 2 * pos), F32),
            dma((2, 2, n)),
            dma((2, 2, n)),
            dma((2, n + 1)),
            dma((2, n + 1)),
            dma((2, n + 1)),
            dma((2, n + 1)),
            dma((2, 2, n)),
            dma((2, 2, n)),
            dma((2, count)),
            dma((2, count)),
        ],
        compiler_params=pltpu.CompilerParams(
            collective_id=0, has_side_effects=True, vmem_limit_bytes=48 * 1024 * 1024
        ),
    )(
        tokens.reshape(part, width),
        cotangent.reshape(part, width),
        gain[None],
        w_qkv.transpose(1, 0, 2),
        w_proj,
        bias,
        mask,
    )
    if not direct:
        wsum = lax.psum_scatter(wsum, ("row", "col"), scatter_dimension=1, tiled=True) * scale
        tall = lax.psum(tall, ("row", "col"))
    summed = tall.reshape(pairs, pos, 2, pos).transpose(1, 3, 0, 2).reshape(pos * pos, heads)
    table_grad = jnp.dot(onehot.T, summed, precision=HIGH) * (WIN * scale)
    return (
        mixed.reshape(part_rows, ncol, width),
        token_gradient.reshape(part_rows, ncol, width),
        wsum,
        table_grad,
    )


def solution(mesh):
    n, nr, nc = (mesh.shape[name] for name in ("head", "row", "col"))
    return jax.shard_map(
        functools.partial(on_device, n, nr, nc),
        mesh=mesh,
        in_specs=(
            P(("row", "head"), "col", None),
            P("row", "col"),
            P(),
            P(None, None, "head"),
            P("head", None),
            P(None, "head"),
            P(("row", "head"), "col", None),
        ),
        out_specs=(
            P(("row", "head"), "col", None),
            P(("row", "head"), "col", None),
            P("head", ("row", "col")),
            P(None, "head"),
        ),
        check_vma=False,
    )
```

```python
import functools
import math

import jax
import jax.numpy as jnp
from jax import lax
from jax.experimental import pallas as pl
from jax.experimental.pallas import tpu as pltpu
from jax.sharding import PartitionSpec as P

HD = 64
WIN = 8
SHIFT = 4
UNIT = SHIFT * SHIFT
EPS = 1e-05
HIGH = lax.Precision.HIGHEST
MESH = pl.DeviceIdType.MESH
F32 = jnp.float32
BF16 = jnp.bfloat16
NN = (((1,), (0,)), ((), ()))
NT = (((1,), (1,)), ((), ()))
TN = (((0,), (0,)), ((), ()))


def dot(a, b, dims):
    return lax.dot_general(a, b, dims, preferred_element_type=F32)


def region(index, grand_total):
    return jnp.where(
        index < grand_total - WIN, 0, jnp.where(index < grand_total - SHIFT, 1, 2)
    ).astype(jnp.int32)


def window_places():
    pos = jnp.arange(WIN * WIN, dtype=jnp.int32)
    prow = pos // 32 * SHIFT + pos // SHIFT % SHIFT
    pcol = pos // 16 % 2 * SHIFT + pos % SHIFT
    return prow, pcol


def offsets():
    span = 2 * WIN - 1
    prow, pcol = window_places()
    index = (prow[:, None] - prow[None, :] + WIN - 1) * span + (
        pcol[:, None] - pcol[None, :] + WIN - 1
    )
    table_ids = jnp.arange(span * span, dtype=jnp.int32)
    return (
        (index[:, :, None] == table_ids[None, None, :])
        .astype(F32)
        .reshape(WIN * WIN * WIN * WIN, span * span)
    )


def kernel(
    sizes,
    tok_ref, cot_ref, gain_ref, wq_ref, wp_ref, bias_ref, mask_ref,
    mixed_ref, tg_ref, pg_ref, ts_ref,
    xhat, rstd, gath, tile_q, tile_g, back_a, back_d, probs, terms, recv, wsend, wrecv, tsend, trecv, tsum,
    ag_send, ag_recv, in_send, in_recv, out_send, out_recv, rs_send, rs_recv,
    pl_send, pl_recv,
):
    n, nr, nc, plane, direct, ncol, pg_scale = sizes
    h = lax.axis_index("head")
    r = lax.axis_index("row")
    c = lax.axis_index("col")
    part, width = tok_ref.shape
    group = wp_ref.shape[0]
    ucols = part // UNIT
    COT, NORM = 0, 1

    def at(dr, dc):
        return {"row": lax.rem(r + dr % nr, nr), "col": lax.rem(c + dc % nc, nc)}

    barrier = pltpu.get_barrier_semaphore()
    for dr, dc in plane:
        pl.semaphore_signal(barrier, inc=1, device_id=at(dr, dc), device_id_type=MESH)
    for dh in (1, n - 1):
        pl.semaphore_signal(
            barrier, inc=1, device_id={"head": lax.rem(h + dh, n)}, device_id_type=MESH
        )

    unit_at = lax.broadcasted_iota(jnp.int32, (part, part), 0)
    patch_at = lax.broadcasted_iota(jnp.int32, (part, part), 1)
    wanted = unit_at // SHIFT % SHIFT * ncol + unit_at // UNIT * SHIFT + unit_at % SHIFT
    perm = jnp.where(wanted == patch_at, 1.0, 0.0).astype(BF16)

    x = dot(perm, tok_ref[...], NN)
    cen = x - jnp.mean(x, -1, keepdims=True)
    inv = lax.rsqrt(jnp.mean(cen * cen, -1, keepdims=True) + EPS)
    std = cen * inv
    xhat[...] = std
    rstd[...] = inv
    gath[NORM, h] = (std * gain_ref[...]).astype(BF16)
    gath[COT, h] = dot(perm, cot_ref[...], NN).astype(BF16)
    pl.semaphore_wait(barrier, len(plane) + 2)

    def ag_copy(arr, way, t, blk):
        step = 1 - 2 * way
        return pltpu.make_async_remote_copy(
            src_ref=gath.at[arr, blk], dst_ref=gath.at[arr, blk],
            send_sem=ag_send.at[arr, way, t], recv_sem=ag_recv.at[arr, way, t],
            device_id={"head": h + step}, device_id_type=MESH,
        )

    def sends(way, t):
        if way == 0:
            return (h < n - 1) & (h >= t)
        return (h > 0) & (h < n - t)

    short = jnp.minimum(h, n - 1 - h)

    def arrival(k):
        paired = k <= 2 * short
        way = jnp.where(paired, lax.rem(k - 1, 2), jnp.where(2 * h > n - 1, 0, 1))
        t = jnp.where(paired, (k - 1) // 2, k - 1 - short)
        return way, t, 1 - 2 * way

    def arrived_block(k):
        way, t, step = arrival(k)
        return jnp.where(k == 0, h, h - step * (t + 1))

    def can_send(way):
        return jnp.where(way == 0, h < n - 1, h > 0)

    def receive(arr, k):
        way, t, step = arrival(k)
        blk = h - step * (t + 1)
        pltpu.make_async_remote_copy(
            src_ref=gath.at[arr, blk], dst_ref=gath.at[arr, blk],
            send_sem=ag_send.at[arr, way, t], recv_sem=ag_recv.at[arr, way, t],
            device_id={"head": h - step}, device_id_type=MESH,
        ).wait_recv()

        @pl.when(can_send(way))
        def _():
            ag_copy(arr, way, t + 1, blk).start()

        if arr == NORM:
            last = t + 1 == jnp.where(way == 0, h, n - 1 - h)

            @pl.when(last & can_send(way))
            def _():
                ag_copy(COT, way, 0, h).start()

    def in_copy(kind, k):
        tile = (tile_q, tile_g)[kind]
        if k == 0:
            src, dst, dev = tile.at[0, pl.ds(1, ucols - 1)], tile.at[n, pl.ds(1, ucols - 1)], at(-1, 0)
        elif k == n:
            src, dst, dev = tile.at[0, 0], tile.at[n, ucols], at(-1, -1)
        else:
            src, dst, dev = tile.at[k, 0], tile.at[k, ucols], at(0, -1)
        return pltpu.make_async_remote_copy(
            src_ref=src, dst_ref=dst, send_sem=in_send.at[kind, k], recv_sem=in_recv.at[kind, k],
            device_id=dev, device_id_type=MESH,
        )

    def project(kind, blk):
        if kind == 0:
            for s in range(3):
                out = dot(gath[NORM, blk], wq_ref[s], NN).astype(BF16)
                tile_q[blk, pl.ds(0, ucols), :, pl.ds(s * group, group)] = out.reshape(
                    ucols, UNIT, group
                )
        else:
            out = dot(gath[COT, blk], wp_ref[...], NT).astype(BF16)
            tile_g[blk, pl.ds(0, ucols)] = out.reshape(ucols, UNIT, group)
        for k in range(n):
            @pl.when(blk == k)
            def _():
                in_copy(kind, k).start()
                if k == 0:
                    in_copy(kind, n).start()

    for way in range(2):
        @pl.when(sends(way, 0))
        def _():
            ag_copy(NORM, way, 0, h).start()

        @pl.when(h == (0, n - 1)[way])
        def _():
            ag_copy(COT, way, 0, h).start()

    @pl.loop(0, n)
    def _(k):
        @pl.when(k > 0)
        def _():
            receive(NORM, k)

        project(0, arrived_block(k))

    for k in range(n + 1):
        in_copy(0, k).wait_recv()

    lane = lax.broadcasted_iota(jnp.int32, (2 * WIN * WIN, 2 * HD), 1)
    first = lane < HD
    keep0 = jnp.where(first, 1.0, 0.0).astype(BF16)
    keep1 = jnp.where(first, 0.0, 1.0).astype(BF16)
    half = 2 * WIN * WIN
    scale = HD ** (-0.5)
    heads2 = group // (2 * HD)
    pairs2 = ucols // 4

    def places(i, jp):
        return [(2 * i + 1 + ur, 4 * jp + 1 + 2 * w) for w in range(2) for ur in range(2)]

    def load(tile, i, jp, at_lane):
        return jnp.concatenate(
            [
                tile[ur, pl.ds(uc, 2), :, pl.ds(at_lane, 2 * HD)].reshape(2 * UNIT, 2 * HD)
                for ur, uc in places(i, jp)
            ],
            0,
        )

    def save(tile, i, jp, at_lane, value):
        for k, (ur, uc) in enumerate(places(i, jp)):
            tile[ur, pl.ds(uc, 2), :, pl.ds(at_lane, 2 * HD)] = (
                value[2 * UNIT * k : 2 * UNIT * (k + 1)].astype(BF16).reshape(2, UNIT, 2 * HD)
            )

    def both(value):
        return jnp.concatenate([value * keep0, value * keep1], 0)

    def chosen(value):
        return jnp.where(first, value[:half], value[half:])

    def forward(i, jp):
        for hp in range(heads2):
            base = hp * 2 * HD
            q, k, v = [load(tile_q, i, jp, base + s * group) for s in range(3)]
            m = mask_ref[pairs2 * i + jp]
            s = dot(both(q), k, NT) * scale + bias_ref[hp] + jnp.concatenate([m, m], 0)
            e = jnp.exp(s - jnp.max(s, -1, keepdims=True))
            p = e / jnp.sum(e, -1, keepdims=True)
            probs[pairs2 * i + jp, hp] = p
            save(back_a, i, jp, base, chosen(dot(p.astype(BF16), v, NN)))

    def backward(i, jp):
        for hp in range(heads2):
            base = hp * 2 * HD
            q, k, v = [load(tile_q, i, jp, base + s * group) for s in range(3)]
            dos = both(load(tile_g, i, jp, base))
            p = probs[pairs2 * i + jp, hp]
            dp = dot(dos, v, NT)
            save(back_d, i, jp, base + 2 * group, dot(p.astype(BF16), dos, TN))
            ds = p * (dp - jnp.sum(p * dp, -1, keepdims=True))
            dsb = ds.astype(BF16)
            save(back_d, i, jp, base, chosen(dot(dsb, k, NN) * scale))
            save(back_d, i, jp, base + group, dot(dsb, both(q), TN) * scale)
            tsum[hp] += ds

    def out_copy(kind, k):
        back = (back_a, back_d)[kind]
        if k == 0:
            src, dst, dev = back.at[n, pl.ds(1, ucols - 1)], back.at[0, pl.ds(1, ucols - 1)], at(1, 0)
        elif k == n:
            src, dst, dev = back.at[n, ucols], back.at[0, 0], at(1, 1)
        else:
            src, dst, dev = back.at[k, ucols], back.at[k, 0], at(0, 1)
        return pltpu.make_async_remote_copy(
            src_ref=src, dst_ref=dst, send_sem=out_send.at[kind, k], recv_sem=out_recv.at[kind, k],
            device_id=dev, device_id_type=MESH,
        )

    def windows(kind, step, between):
        @pl.loop(0, n // 2 * pairs2)
        def _(count):
            i = n // 2 - 1 - count // pairs2
            jp = pairs2 - 1 - lax.rem(count, pairs2)
            step(i, jp)
            for i_at in range(n // 2):
                @pl.when((i == i_at) & (jp == pairs2 - 1))
                def _():
                    out_copy(kind, 2 * i_at + 1).start()
                    out_copy(kind, 2 * i_at + 2).start()

            @pl.when((i == n // 2 - 1) & (jp == 0))
            def _():
                out_copy(kind, 0).start()

            between(count)

    def between_forward(count):
        @pl.when(count < n - 2)
        def _():
            receive(COT, count + 1)

    windows(0, forward, between_forward)
    for k in range(n + 1):
        out_copy(0, k).wait_recv()

    def block(back, d):
        return back[d, pl.ds(0, ucols)].reshape(part, back.shape[-1])

    def rs_copy(arr, way, d):
        step = 1 - 2 * way
        return pltpu.make_async_remote_copy(
            src_ref=terms.at[arr, d], dst_ref=recv.at[arr, way, d],
            send_sem=rs_send.at[arr, way, d], recv_sem=rs_recv.at[arr, way, d],
            device_id={"head": h + step}, device_id_type=MESH,
        )

    def rs_arrived(arr, way, d):
        step = 1 - 2 * way
        pltpu.make_async_remote_copy(
            src_ref=terms.at[arr, d], dst_ref=recv.at[arr, way, d],
            send_sem=rs_send.at[arr, way, d], recv_sem=rs_recv.at[arr, way, d],
            device_id={"head": h - step}, device_id_type=MESH,
        ).wait_recv()

    def order(k):
        return jnp.where(lax.rem(k, 2) == 0, n - 1 - k // 2, k // 2)

    def rs_start(arr):
        @pl.loop(0, n)
        def _(k):
            d = order(k)
            if arr == 0:
                term = dot(block(back_a, d), wp_ref[...], NN)
            else:
                grads = block(back_d, d)
                term = sum(
                    dot(grads[:, s * group : (s + 1) * group], wq_ref[s], NT) for s in range(3)
                )
            terms[arr, d] = term.astype(BF16)

            @pl.when((h == 0) & (d > 0))
            def _():
                rs_copy(arr, 0, d).start()

            @pl.when((h == n - 1) & (d < n - 1))
            def _():
                rs_copy(arr, 1, d).start()

    def rs_transit(arr, k):
        d = order(k)

        @pl.when(((h < d) & (h > 0)) | ((h > d) & (h < n - 1)))
        def _():
            way = jnp.where(h < d, 0, 1)
            rs_arrived(arr, way, d)
            terms[arr, d] = (terms[arr, d].astype(F32) + recv[arr, way, d].astype(F32)).astype(BF16)
            rs_copy(arr, way, d).start()

    def total(arr):
        sides = [h > 0, h < n - 1]
        for way in range(2):
            @pl.when(sides[way])
            def _():
                rs_arrived(arr, way, h)

            @pl.when(jnp.logical_not(sides[way]))
            def _():
                recv[arr, way, h] = jnp.zeros((part, width), BF16)
        return (
            terms[arr, h].astype(F32) + recv[arr, 0, h].astype(F32) + recv[arr, 1, h].astype(F32)
        )

    rs_start(0)

    @pl.loop(0, n)
    def _(k):
        @pl.when(k == n - 1)
        def _():
            receive(COT, k)

        project(1, arrived_block(k))

    for k in range(n + 1):
        in_copy(1, k).wait_recv()

    tsum[...] = jnp.zeros_like(tsum)
    windows(1, backward, functools.partial(rs_transit, 0))

    low = lax.broadcasted_iota(jnp.int32, (WIN * WIN, 2 * HD), 1) < HD
    for hp in range(heads2):
        folds = []
        for k in range(2):
            f = tsum[hp, k * half : k * half + HD] + tsum[hp, k * half + HD : (k + 1) * half]
            folds.append(f + pltpu.roll(f, HD, 1))
        tsend[hp] = jnp.where(low, folds[0], folds[1])

    for k in range(n + 1):
        out_copy(1, k).wait_recv()
    rs_start(1)

    def pl_copy(kind, o):
        dr, dc = plane[o]
        there = at(dr, dc)
        if kind == 0:
            src, dst = wsend.at[there["row"] * nc + there["col"]], wrecv.at[o]
        else:
            src, dst = tsend, trecv.at[o]
        return pltpu.make_async_remote_copy(
            src_ref=src, dst_ref=dst, send_sem=pl_send.at[kind, o], recv_sem=pl_recv.at[kind, o],
            device_id=there, device_id_type=MESH,
        )

    wide = 2 * 128

    @pl.loop(0, width // wide)
    def _(j):
        attn = back_a[pl.ds(0, n), pl.ds(0, ucols)].reshape(n * part, group)
        cols = pl.ds(pl.multiple_of(j * wide, wide), wide)
        wterm = dot(attn, gath[COT, :, :, cols].reshape(n * part, wide), TN)
        if direct:
            piece = width // (nr * nc)
            for k in range(wide // piece):
                wsend[wide // piece * j + k] = wterm[:, k * piece : (k + 1) * piece].astype(BF16)
        else:
            pg_ref[:, cols] = wterm

    if direct:
        for o in range(len(plane)):
            for kind in range(2):
                pl_copy(kind, o).start()
    else:
        ts_ref[...] = tsend[...]

    @pl.loop(0, n)
    def _(k):
        rs_transit(1, k)

    mixed = dot(perm, tok_ref[...], NN) + total(0)
    mixed_ref[...] = dot(perm, mixed.astype(BF16), TN).astype(BF16)

    if direct:
        for o in range(len(plane)):
            for kind in range(2):
                pl_copy(kind, o).wait_recv()
        wsum = wsend[r * nc + c].astype(F32)
        tall = tsend[...]
        for o in range(len(plane)):
            wsum = wsum + wrecv[o].astype(F32)
            tall = tall + trecv[o]
        pg_ref[...] = wsum * pg_scale
        ts_ref[...] = tall
        for o in range(len(plane)):
            for kind in range(2):
                pl_copy(kind, o).wait_send()

    gg = total(1) * gain_ref[...]
    std = xhat[...]
    tg = gath[COT, h].astype(F32) + rstd[...] * (
        gg - jnp.mean(gg, -1, keepdims=True) - std * jnp.mean(gg * std, -1, keepdims=True)
    )
    tg_ref[...] = dot(perm, tg.astype(BF16), TN).astype(BF16)

    for arr in range(2):
        for way in range(2):
            for t in range(n - 1):
                @pl.when(sends(way, t))
                def _():
                    ag_copy(arr, way, t, h - (1 - 2 * way) * t).wait_send()
    for kind in range(2):
        for k in range(n + 1):
            in_copy(kind, k).wait_send()
            out_copy(kind, k).wait_send()
    for arr in range(2):
        for d in range(n):
            if d > 0:
                @pl.when(h < d)
                def _():
                    rs_copy(arr, 0, d).wait_send()
            if d < n - 1:
                @pl.when(h > d)
                def _():
                    rs_copy(arr, 1, d).wait_send()


def on_device(n, nr, nc, tokens, valid, gain, w_qkv, w_proj, rel_table, cotangent):
    part_rows, ncol, width = tokens.shape
    tile_rows = part_rows * n
    part = part_rows * ncol
    heads = rel_table.shape[1]
    group = heads * HD
    pairs = heads // 2
    pos = WIN * WIN
    ucols = ncol // SHIFT

    row_lab = region(
        lax.axis_index("row") * tile_rows + jnp.arange(tile_rows, dtype=jnp.int32), tile_rows * nr
    )
    col_lab = region(lax.axis_index("col") * ncol + jnp.arange(ncol, dtype=jnp.int32), ncol * nc)
    labels = 3 * row_lab[:, None] + col_lab[None, :]

    def to_pairs(block):
        block = block.reshape(tile_rows // WIN, 2, SHIFT, ncol // WIN, 2, SHIFT)
        return block.transpose(0, 3, 1, 4, 2, 5).reshape(-1, 2 * pos)

    lab = to_pairs(labels) + 16 * (jnp.arange(2 * pos, dtype=jnp.int32) // pos)[None]
    val = to_pairs(valid)
    allowed = (lab[:, :, None] == lab[:, None, :]) & (
        (val[:, None, :] == 1) | jnp.eye(2 * pos, dtype=bool)[None]
    )
    mask = jnp.where(allowed, 0.0, -1e30).astype(F32)
    onehot = offsets()
    bias = jnp.dot(onehot, rel_table, precision=HIGH).reshape(pos, pos, heads).transpose(2, 0, 1)
    bias = jnp.broadcast_to(
        bias.reshape(pairs, 2, 1, pos, 1, pos), (pairs, 2, 2, pos, 2, pos)
    ).reshape(pairs, 4 * pos, 2 * pos)

    scale = 1.0 / math.sqrt(tile_rows * ncol * nr * nc)
    direct = nr * nc <= 8
    if direct:
        plane = [(dr, dc) for dr in range(nr) for dc in range(nc) if (dr, dc) != (0, 0)]
    else:
        six = [(1, 0), (nr - 1, 0), (0, 1), (0, nc - 1), (1, 1), (nr - 1, nc - 1)]
        plane = sorted(set(six))
    count = len(plane)
    piece = width // (nr * nc)
    vmem = pl.BlockSpec(memory_space=pltpu.VMEM)
    dma = pltpu.SemaphoreType.DMA
    mixed, token_gradient, wsum, tall = pl.pallas_call(
        functools.partial(kernel, (n, nr, nc, tuple(plane), direct, ncol, scale)),
        out_shape=(
            jax.ShapeDtypeStruct((part, width), BF16),
            jax.ShapeDtypeStruct((part, width), BF16),
            jax.ShapeDtypeStruct((group, piece if direct else width), F32),
            jax.ShapeDtypeStruct((pairs, pos, 2 * HD), F32),
        ),
        in_specs=[vmem] * 7,
        out_specs=[vmem] * 4,
        scratch_shapes=[
            pltpu.VMEM((part, width), F32),
            pltpu.VMEM((part, 1), F32),
            pltpu.VMEM((2, n, part, width), BF16),
            pltpu.VMEM((n + 1, ucols + 1, UNIT, 3 * group), BF16),
            pltpu.VMEM((n + 1, ucols + 1, UNIT, group), BF16),
            pltpu.VMEM((n + 1, ucols + 1, UNIT, group), BF16),
            pltpu.VMEM((n + 1, ucols + 1, UNIT, 3 * group), BF16),
            pltpu.VMEM((n * ucols // 8, pairs, 4 * pos, 2 * pos), F32),
            pltpu.VMEM((2, n, part, width), BF16),
            pltpu.VMEM((2, 2, n, part, width), BF16),
            pltpu.VMEM((nr * nc, group, piece) if direct else (1, 16, 128), BF16),
            pltpu.VMEM((count, group, piece) if direct else (1, 16, 128), BF16),
            pltpu.VMEM((pairs, pos, 2 * HD), F32),
            pltpu.VMEM((count, pairs, pos, 2 * HD) if direct else (1, 16, 128), F32),
            pltpu.VMEM((pairs, 4 * pos, 2 * pos), F32),
            dma((2, 2, n)),
            dma((2, 2, n)),
            dma((2, n + 1)),
            dma((2, n + 1)),
            dma((2, n + 1)),
            dma((2, n + 1)),
            dma((2, 2, n)),
            dma((2, 2, n)),
            dma((2, count)),
            dma((2, count)),
        ],
        compiler_params=pltpu.CompilerParams(
            collective_id=0, has_side_effects=True, vmem_limit_bytes=48 * 1024 * 1024
        ),
    )(
        tokens.reshape(part, width),
        cotangent.reshape(part, width),
        gain[None],
        w_qkv.transpose(1, 0, 2),
        w_proj,
        bias,
        mask,
    )
    if not direct:
        wsum = lax.psum_scatter(wsum, ("row", "col"), scatter_dimension=1, tiled=True) * scale
        tall = lax.psum(tall, ("row", "col"))
    summed = tall.reshape(pairs, pos, 2, pos).transpose(1, 3, 0, 2).reshape(pos * pos, heads)
    table_grad = jnp.dot(onehot.T, summed, precision=HIGH) * (WIN * scale)
    return (
        mixed.reshape(part_rows, ncol, width),
        token_gradient.reshape(part_rows, ncol, width),
        wsum,
        table_grad,
    )


def solution(mesh):
    n, nr, nc = (mesh.shape[name] for name in ("head", "row", "col"))
    return jax.shard_map(
        functools.partial(on_device, n, nr, nc),
        mesh=mesh,
        in_specs=(
            P(("row", "head"), "col", None),
            P("row", "col"),
            P(),
            P(None, None, "head"),
            P("head", None),
            P(None, "head"),
            P(("row", "head"), "col", None),
        ),
        out_specs=(
            P(("row", "head"), "col", None),
            P(("row", "head"), "col", None),
            P("head", ("row", "col")),
            P(None, "head"),
        ),
        check_vma=False,
    )
```

```python
import functools
import math

import jax
import jax.numpy as jnp
from jax import lax
from jax.experimental import pallas as pl
from jax.experimental.pallas import tpu as pltpu
from jax.sharding import PartitionSpec as P

HD = 64
WIN = 8
SHIFT = 4
UNIT = SHIFT * SHIFT
EPS = 1e-05
HIGH = lax.Precision.HIGHEST
MESH = pl.DeviceIdType.MESH
F32 = jnp.float32
BF16 = jnp.bfloat16
NN = (((1,), (0,)), ((), ()))
NT = (((1,), (1,)), ((), ()))
TN = (((0,), (0,)), ((), ()))


def dot(a, b, dims):
    return lax.dot_general(a, b, dims, preferred_element_type=F32)


def region(index, grand_total):
    return jnp.where(
        index < grand_total - WIN, 0, jnp.where(index < grand_total - SHIFT, 1, 2)
    ).astype(jnp.int32)


def window_places():
    pos = jnp.arange(WIN * WIN, dtype=jnp.int32)
    prow = pos // 32 * SHIFT + pos // SHIFT % SHIFT
    pcol = pos // 16 % 2 * SHIFT + pos % SHIFT
    return prow, pcol


def offsets():
    span = 2 * WIN - 1
    prow, pcol = window_places()
    index = (prow[:, None] - prow[None, :] + WIN - 1) * span + (
        pcol[:, None] - pcol[None, :] + WIN - 1
    )
    table_ids = jnp.arange(span * span, dtype=jnp.int32)
    return (
        (index[:, :, None] == table_ids[None, None, :])
        .astype(F32)
        .reshape(WIN * WIN * WIN * WIN, span * span)
    )


def kernel(
    sizes,
    tok_ref, cot_ref, gain_ref, wq_ref, wp_ref, bias_ref, mask_ref,
    mixed_ref, tg_ref, pg_ref, ts_ref,
    xhat, rstd, gath, tile_q, tile_g, back_a, back_d, probs, terms, recv, wsend, wrecv, tsend, trecv, tsum,
    ag_send, ag_recv, in_send, in_recv, out_send, out_recv, rs_send, rs_recv,
    pl_send, pl_recv,
):
    n, nr, nc, plane, direct, ncol, pg_scale = sizes
    h = lax.axis_index("head")
    r = lax.axis_index("row")
    c = lax.axis_index("col")
    part, width = tok_ref.shape
    group = wp_ref.shape[0]
    ucols = part // UNIT
    COT, NORM = 0, 1

    def at(dr, dc):
        return {"row": lax.rem(r + dr % nr, nr), "col": lax.rem(c + dc % nc, nc)}

    barrier = pltpu.get_barrier_semaphore()
    for dr, dc in plane:
        pl.semaphore_signal(barrier, inc=1, device_id=at(dr, dc), device_id_type=MESH)
    for dh in (1, n - 1):
        pl.semaphore_signal(
            barrier, inc=1, device_id={"head": lax.rem(h + dh, n)}, device_id_type=MESH
        )

    unit_at = lax.broadcasted_iota(jnp.int32, (part, part), 0)
    patch_at = lax.broadcasted_iota(jnp.int32, (part, part), 1)
    wanted = unit_at // SHIFT % SHIFT * ncol + unit_at // UNIT * SHIFT + unit_at % SHIFT
    perm = jnp.where(wanted == patch_at, 1.0, 0.0).astype(BF16)

    x = dot(perm, tok_ref[...], NN)
    cen = x - jnp.mean(x, -1, keepdims=True)
    inv = lax.rsqrt(jnp.mean(cen * cen, -1, keepdims=True) + EPS)
    std = cen * inv
    xhat[...] = std
    rstd[...] = inv
    gath[NORM, h] = (std * gain_ref[...]).astype(BF16)
    gath[COT, h] = dot(perm, cot_ref[...], NN).astype(BF16)
    pl.semaphore_wait(barrier, len(plane) + 2)

    def ag_copy(arr, way, t, blk):
        step = 1 - 2 * way
        return pltpu.make_async_remote_copy(
            src_ref=gath.at[arr, blk], dst_ref=gath.at[arr, blk],
            send_sem=ag_send.at[arr, way, t], recv_sem=ag_recv.at[arr, way, t],
            device_id={"head": h + step}, device_id_type=MESH,
        )

    def sends(way, t):
        if way == 0:
            return (h < n - 1) & (h >= t)
        return (h > 0) & (h < n - t)

    short = jnp.minimum(h, n - 1 - h)

    def arrival(k):
        paired = k <= 2 * short
        way = jnp.where(paired, lax.rem(k - 1, 2), jnp.where(2 * h > n - 1, 0, 1))
        t = jnp.where(paired, (k - 1) // 2, k - 1 - short)
        return way, t, 1 - 2 * way

    def arrived_block(k):
        way, t, step = arrival(k)
        return jnp.where(k == 0, h, h - step * (t + 1))

    def can_send(way):
        return jnp.where(way == 0, h < n - 1, h > 0)

    def receive(arr, k):
        way, t, step = arrival(k)
        blk = h - step * (t + 1)
        pltpu.make_async_remote_copy(
            src_ref=gath.at[arr, blk], dst_ref=gath.at[arr, blk],
            send_sem=ag_send.at[arr, way, t], recv_sem=ag_recv.at[arr, way, t],
            device_id={"head": h - step}, device_id_type=MESH,
        ).wait_recv()

        @pl.when(can_send(way))
        def _():
            ag_copy(arr, way, t + 1, blk).start()

        if arr == NORM:
            last = t + 1 == jnp.where(way == 0, h, n - 1 - h)

            @pl.when(last & can_send(way))
            def _():
                ag_copy(COT, way, 0, h).start()

    def in_copy(kind, k):
        tile = (tile_q, tile_g)[kind]
        if k == 0:
            src, dst, dev = tile.at[0, pl.ds(1, ucols - 1)], tile.at[n, pl.ds(1, ucols - 1)], at(-1, 0)
        elif k == n:
            src, dst, dev = tile.at[0, 0], tile.at[n, ucols], at(-1, -1)
        else:
            src, dst, dev = tile.at[k, 0], tile.at[k, ucols], at(0, -1)
        return pltpu.make_async_remote_copy(
            src_ref=src, dst_ref=dst, send_sem=in_send.at[kind, k], recv_sem=in_recv.at[kind, k],
            device_id=dev, device_id_type=MESH,
        )

    def project(kind, blk):
        if kind == 0:
            for s in range(3):
                out = dot(gath[NORM, blk], wq_ref[s], NN).astype(BF16)
                tile_q[blk, pl.ds(0, ucols), :, pl.ds(s * group, group)] = out.reshape(
                    ucols, UNIT, group
                )
        else:
            out = dot(gath[COT, blk], wp_ref[...], NT).astype(BF16)
            tile_g[blk, pl.ds(0, ucols)] = out.reshape(ucols, UNIT, group)
        for k in range(n):
            @pl.when(blk == k)
            def _():
                in_copy(kind, k).start()
                if k == 0:
                    in_copy(kind, n).start()

    for way in range(2):
        @pl.when(sends(way, 0))
        def _():
            ag_copy(NORM, way, 0, h).start()

        @pl.when(h == (0, n - 1)[way])
        def _():
            ag_copy(COT, way, 0, h).start()

    @pl.loop(0, n)
    def _(k):
        @pl.when(k > 0)
        def _():
            receive(NORM, k)

        project(0, arrived_block(k))

    for k in range(n + 1):
        in_copy(0, k).wait_recv()

    lane = lax.broadcasted_iota(jnp.int32, (2 * WIN * WIN, 2 * HD), 1)
    first = lane < HD
    keep0 = jnp.where(first, 1.0, 0.0).astype(BF16)
    keep1 = jnp.where(first, 0.0, 1.0).astype(BF16)
    half = 2 * WIN * WIN
    scale = HD ** (-0.5)
    heads2 = group // (2 * HD)
    pairs2 = ucols // 4

    def places(i, jp):
        return [(2 * i + 1 + ur, 4 * jp + 1 + 2 * w) for w in range(2) for ur in range(2)]

    def load(tile, i, jp, at_lane):
        return jnp.concatenate(
            [
                tile[ur, pl.ds(uc, 2), :, pl.ds(at_lane, 2 * HD)].reshape(2 * UNIT, 2 * HD)
                for ur, uc in places(i, jp)
            ],
            0,
        )

    def save(tile, i, jp, at_lane, value):
        for k, (ur, uc) in enumerate(places(i, jp)):
            tile[ur, pl.ds(uc, 2), :, pl.ds(at_lane, 2 * HD)] = (
                value[2 * UNIT * k : 2 * UNIT * (k + 1)].astype(BF16).reshape(2, UNIT, 2 * HD)
            )

    def both(value):
        return jnp.concatenate([value * keep0, value * keep1], 0)

    def chosen(value):
        return jnp.where(first, value[:half], value[half:])

    def forward(i, jp):
        for hp in range(heads2):
            base = hp * 2 * HD
            q, k, v = [load(tile_q, i, jp, base + s * group) for s in range(3)]
            m = mask_ref[pairs2 * i + jp]
            s = dot(both(q), k, NT) * scale + bias_ref[hp] + jnp.concatenate([m, m], 0)
            e = jnp.exp(s - jnp.max(s, -1, keepdims=True))
            p = e / jnp.sum(e, -1, keepdims=True)
            probs[pairs2 * i + jp, hp] = p
            save(back_a, i, jp, base, chosen(dot(p.astype(BF16), v, NN)))

    def backward(i, jp):
        for hp in range(heads2):
            base = hp * 2 * HD
            q, k, v = [load(tile_q, i, jp, base + s * group) for s in range(3)]
            dos = both(load(tile_g, i, jp, base))
            p = probs[pairs2 * i + jp, hp]
            dp = dot(dos, v, NT)
            save(back_d, i, jp, base + 2 * group, dot(p.astype(BF16), dos, TN))
            ds = p * (dp - jnp.sum(p * dp, -1, keepdims=True))
            dsb = ds.astype(BF16)
            save(back_d, i, jp, base, chosen(dot(dsb, k, NN) * scale))
            save(back_d, i, jp, base + group, dot(dsb, both(q), TN) * scale)
            tsum[hp] += ds

    def out_copy(kind, k):
        back = (back_a, back_d)[kind]
        if k == 0:
            src, dst, dev = back.at[n, pl.ds(1, ucols - 1)], back.at[0, pl.ds(1, ucols - 1)], at(1, 0)
        elif k == n:
            src, dst, dev = back.at[n, ucols], back.at[0, 0], at(1, 1)
        else:
            src, dst, dev = back.at[k, ucols], back.at[k, 0], at(0, 1)
        return pltpu.make_async_remote_copy(
            src_ref=src, dst_ref=dst, send_sem=out_send.at[kind, k], recv_sem=out_recv.at[kind, k],
            device_id=dev, device_id_type=MESH,
        )

    def windows(kind, step, between):
        @pl.loop(0, n // 2 * pairs2)
        def _(count):
            i = n // 2 - 1 - count // pairs2
            jp = pairs2 - 1 - lax.rem(count, pairs2)
            step(i, jp)
            for i_at in range(n // 2):
                @pl.when((i == i_at) & (jp == pairs2 - 1))
                def _():
                    out_copy(kind, 2 * i_at + 1).start()
                    out_copy(kind, 2 * i_at + 2).start()

            @pl.when((i == n // 2 - 1) & (jp == 0))
            def _():
                out_copy(kind, 0).start()

            between(count)

    def between_forward(count):
        @pl.when(count < n - 2)
        def _():
            receive(COT, count + 1)

    windows(0, forward, between_forward)
    for k in range(n + 1):
        out_copy(0, k).wait_recv()

    def block(back, d):
        return back[d, pl.ds(0, ucols)].reshape(part, back.shape[-1])

    def rs_copy(arr, way, d):
        step = 1 - 2 * way
        return pltpu.make_async_remote_copy(
            src_ref=terms.at[arr, d], dst_ref=recv.at[arr, way, d],
            send_sem=rs_send.at[arr, way, d], recv_sem=rs_recv.at[arr, way, d],
            device_id={"head": h + step}, device_id_type=MESH,
        )

    def rs_arrived(arr, way, d):
        step = 1 - 2 * way
        pltpu.make_async_remote_copy(
            src_ref=terms.at[arr, d], dst_ref=recv.at[arr, way, d],
            send_sem=rs_send.at[arr, way, d], recv_sem=rs_recv.at[arr, way, d],
            device_id={"head": h - step}, device_id_type=MESH,
        ).wait_recv()

    def order(k):
        far = n - 1 - k // 2
        near = k // 2
        return jnp.where((lax.rem(k, 2) == 0) == (2 * h < n - 1), far, near)

    def rs_start(arr):
        @pl.loop(0, n)
        def _(k):
            d = order(k)
            if arr == 0:
                term = dot(block(back_a, d), wp_ref[...], NN)
            else:
                grads = block(back_d, d)
                term = sum(
                    dot(grads[:, s * group : (s + 1) * group], wq_ref[s], NT) for s in range(3)
                )
            terms[arr, d] = term.astype(BF16)

            @pl.when((h == 0) & (d > 0))
            def _():
                rs_copy(arr, 0, d).start()

            @pl.when((h == n - 1) & (d < n - 1))
            def _():
                rs_copy(arr, 1, d).start()

    def rs_transit(arr, k):
        d = order(k)

        @pl.when(((h < d) & (h > 0)) | ((h > d) & (h < n - 1)))
        def _():
            way = jnp.where(h < d, 0, 1)
            rs_arrived(arr, way, d)
            terms[arr, d] = (terms[arr, d].astype(F32) + recv[arr, way, d].astype(F32)).astype(BF16)
            rs_copy(arr, way, d).start()

    def total(arr):
        sides = [h > 0, h < n - 1]
        for way in range(2):
            @pl.when(sides[way])
            def _():
                rs_arrived(arr, way, h)

            @pl.when(jnp.logical_not(sides[way]))
            def _():
                recv[arr, way, h] = jnp.zeros((part, width), BF16)
        return (
            terms[arr, h].astype(F32) + recv[arr, 0, h].astype(F32) + recv[arr, 1, h].astype(F32)
        )

    rs_start(0)

    @pl.loop(0, n)
    def _(k):
        @pl.when(k == n - 1)
        def _():
            receive(COT, k)

        project(1, arrived_block(k))

    for k in range(n + 1):
        in_copy(1, k).wait_recv()

    tsum[...] = jnp.zeros_like(tsum)
    def between_backward(count):
        @pl.when(count > 0)
        def _():
            rs_transit(0, count - 1)

    windows(1, backward, between_backward)

    low = lax.broadcasted_iota(jnp.int32, (WIN * WIN, 2 * HD), 1) < HD
    for hp in range(heads2):
        folds = []
        for k in range(2):
            f = tsum[hp, k * half : k * half + HD] + tsum[hp, k * half + HD : (k + 1) * half]
            folds.append(f + pltpu.roll(f, HD, 1))
        tsend[hp] = jnp.where(low, folds[0], folds[1])

    for k in range(n + 1):
        out_copy(1, k).wait_recv()
    rs_start(1)

    def pl_copy(kind, o):
        dr, dc = plane[o]
        there = at(dr, dc)
        if kind == 0:
            src, dst = wsend.at[there["row"] * nc + there["col"]], wrecv.at[o]
        else:
            src, dst = tsend, trecv.at[o]
        return pltpu.make_async_remote_copy(
            src_ref=src, dst_ref=dst, send_sem=pl_send.at[kind, o], recv_sem=pl_recv.at[kind, o],
            device_id=there, device_id_type=MESH,
        )

    wide = 2 * 128

    @pl.loop(0, width // wide)
    def _(j):
        attn = back_a[pl.ds(0, n), pl.ds(0, ucols)].reshape(n * part, group)
        cols = pl.ds(pl.multiple_of(j * wide, wide), wide)
        wterm = dot(attn, gath[COT, :, :, cols].reshape(n * part, wide), TN)
        if direct:
            piece = width // (nr * nc)
            for k in range(wide // piece):
                wsend[wide // piece * j + k] = wterm[:, k * piece : (k + 1) * piece].astype(BF16)
        else:
            pg_ref[:, cols] = wterm

    if direct:
        for o in range(len(plane)):
            for kind in range(2):
                pl_copy(kind, o).start()
    else:
        ts_ref[...] = tsend[...]

    @pl.loop(0, n)
    def _(k):
        rs_transit(1, k)

    mixed = dot(perm, tok_ref[...], NN) + total(0)
    mixed_ref[...] = dot(perm, mixed.astype(BF16), TN).astype(BF16)

    if direct:
        for o in range(len(plane)):
            for kind in range(2):
                pl_copy(kind, o).wait_recv()
        wsum = wsend[r * nc + c].astype(F32)
        tall = tsend[...]
        for o in range(len(plane)):
            wsum = wsum + wrecv[o].astype(F32)
            tall = tall + trecv[o]
        pg_ref[...] = wsum * pg_scale
        ts_ref[...] = tall
        for o in range(len(plane)):
            for kind in range(2):
                pl_copy(kind, o).wait_send()

    gg = total(1) * gain_ref[...]
    std = xhat[...]
    tg = gath[COT, h].astype(F32) + rstd[...] * (
        gg - jnp.mean(gg, -1, keepdims=True) - std * jnp.mean(gg * std, -1, keepdims=True)
    )
    tg_ref[...] = dot(perm, tg.astype(BF16), TN).astype(BF16)

    for arr in range(2):
        for way in range(2):
            for t in range(n - 1):
                @pl.when(sends(way, t))
                def _():
                    ag_copy(arr, way, t, h - (1 - 2 * way) * t).wait_send()
    for kind in range(2):
        for k in range(n + 1):
            in_copy(kind, k).wait_send()
            out_copy(kind, k).wait_send()
    for arr in range(2):
        for d in range(n):
            if d > 0:
                @pl.when(h < d)
                def _():
                    rs_copy(arr, 0, d).wait_send()
            if d < n - 1:
                @pl.when(h > d)
                def _():
                    rs_copy(arr, 1, d).wait_send()


def on_device(n, nr, nc, tokens, valid, gain, w_qkv, w_proj, rel_table, cotangent):
    part_rows, ncol, width = tokens.shape
    tile_rows = part_rows * n
    part = part_rows * ncol
    heads = rel_table.shape[1]
    group = heads * HD
    pairs = heads // 2
    pos = WIN * WIN
    ucols = ncol // SHIFT

    row_lab = region(
        lax.axis_index("row") * tile_rows + jnp.arange(tile_rows, dtype=jnp.int32), tile_rows * nr
    )
    col_lab = region(lax.axis_index("col") * ncol + jnp.arange(ncol, dtype=jnp.int32), ncol * nc)
    labels = 3 * row_lab[:, None] + col_lab[None, :]

    def to_pairs(block):
        block = block.reshape(tile_rows // WIN, 2, SHIFT, ncol // WIN, 2, SHIFT)
        return block.transpose(0, 3, 1, 4, 2, 5).reshape(-1, 2 * pos)

    lab = to_pairs(labels) + 16 * (jnp.arange(2 * pos, dtype=jnp.int32) // pos)[None]
    val = to_pairs(valid)
    allowed = (lab[:, :, None] == lab[:, None, :]) & (
        (val[:, None, :] == 1) | jnp.eye(2 * pos, dtype=bool)[None]
    )
    mask = jnp.where(allowed, 0.0, -1e30).astype(F32)
    onehot = offsets()
    bias = jnp.dot(onehot, rel_table, precision=HIGH).reshape(pos, pos, heads).transpose(2, 0, 1)
    bias = jnp.broadcast_to(
        bias.reshape(pairs, 2, 1, pos, 1, pos), (pairs, 2, 2, pos, 2, pos)
    ).reshape(pairs, 4 * pos, 2 * pos)

    scale = 1.0 / math.sqrt(tile_rows * ncol * nr * nc)
    direct = nr * nc <= 8
    if direct:
        plane = [(dr, dc) for dr in range(nr) for dc in range(nc) if (dr, dc) != (0, 0)]
    else:
        six = [(1, 0), (nr - 1, 0), (0, 1), (0, nc - 1), (1, 1), (nr - 1, nc - 1)]
        plane = sorted(set(six))
    count = len(plane)
    piece = width // (nr * nc)
    vmem = pl.BlockSpec(memory_space=pltpu.VMEM)
    dma = pltpu.SemaphoreType.DMA
    mixed, token_gradient, wsum, tall = pl.pallas_call(
        functools.partial(kernel, (n, nr, nc, tuple(plane), direct, ncol, scale)),
        out_shape=(
            jax.ShapeDtypeStruct((part, width), BF16),
            jax.ShapeDtypeStruct((part, width), BF16),
            jax.ShapeDtypeStruct((group, piece if direct else width), F32),
            jax.ShapeDtypeStruct((pairs, pos, 2 * HD), F32),
        ),
        in_specs=[vmem] * 7,
        out_specs=[vmem] * 4,
        scratch_shapes=[
            pltpu.VMEM((part, width), F32),
            pltpu.VMEM((part, 1), F32),
            pltpu.VMEM((2, n, part, width), BF16),
            pltpu.VMEM((n + 1, ucols + 1, UNIT, 3 * group), BF16),
            pltpu.VMEM((n + 1, ucols + 1, UNIT, group), BF16),
            pltpu.VMEM((n + 1, ucols + 1, UNIT, group), BF16),
            pltpu.VMEM((n + 1, ucols + 1, UNIT, 3 * group), BF16),
            pltpu.VMEM((n * ucols // 8, pairs, 4 * pos, 2 * pos), F32),
            pltpu.VMEM((2, n, part, width), BF16),
            pltpu.VMEM((2, 2, n, part, width), BF16),
            pltpu.VMEM((nr * nc, group, piece) if direct else (1, 16, 128), BF16),
            pltpu.VMEM((count, group, piece) if direct else (1, 16, 128), BF16),
            pltpu.VMEM((pairs, pos, 2 * HD), F32),
            pltpu.VMEM((count, pairs, pos, 2 * HD) if direct else (1, 16, 128), F32),
            pltpu.VMEM((pairs, 4 * pos, 2 * pos), F32),
            dma((2, 2, n)),
            dma((2, 2, n)),
            dma((2, n + 1)),
            dma((2, n + 1)),
            dma((2, n + 1)),
            dma((2, n + 1)),
            dma((2, 2, n)),
            dma((2, 2, n)),
            dma((2, count)),
            dma((2, count)),
        ],
        compiler_params=pltpu.CompilerParams(
            collective_id=0, has_side_effects=True, vmem_limit_bytes=48 * 1024 * 1024
        ),
    )(
        tokens.reshape(part, width),
        cotangent.reshape(part, width),
        gain[None],
        w_qkv.transpose(1, 0, 2),
        w_proj,
        bias,
        mask,
    )
    if not direct:
        wsum = lax.psum_scatter(wsum, ("row", "col"), scatter_dimension=1, tiled=True) * scale
        tall = lax.psum(tall, ("row", "col"))
    summed = tall.reshape(pairs, pos, 2, pos).transpose(1, 3, 0, 2).reshape(pos * pos, heads)
    table_grad = jnp.dot(onehot.T, summed, precision=HIGH) * (WIN * scale)
    return (
        mixed.reshape(part_rows, ncol, width),
        token_gradient.reshape(part_rows, ncol, width),
        wsum,
        table_grad,
    )


def solution(mesh):
    n, nr, nc = (mesh.shape[name] for name in ("head", "row", "col"))
    return jax.shard_map(
        functools.partial(on_device, n, nr, nc),
        mesh=mesh,
        in_specs=(
            P(("row", "head"), "col", None),
            P("row", "col"),
            P(),
            P(None, None, "head"),
            P("head", None),
            P(None, "head"),
            P(("row", "head"), "col", None),
        ),
        out_specs=(
            P(("row", "head"), "col", None),
            P(("row", "head"), "col", None),
            P("head", ("row", "col")),
            P(None, "head"),
        ),
        check_vma=False,
    )
```

```python
import functools
import math

import jax
import jax.numpy as jnp
from jax import lax
from jax.experimental import pallas as pl
from jax.experimental.pallas import tpu as pltpu
from jax.sharding import PartitionSpec as P

HD = 64
WIN = 8
SHIFT = 4
UNIT = SHIFT * SHIFT
EPS = 1e-05
MESH = pl.DeviceIdType.MESH
F32 = jnp.float32
BF16 = jnp.bfloat16
NN = (((1,), (0,)), ((), ()))
NT = (((1,), (1,)), ((), ()))
TN = (((0,), (0,)), ((), ()))


def dot(a, b, dims):
    return lax.dot_general(a, b, dims, preferred_element_type=F32)


def region(index, grand_total):
    return jnp.where(
        index < grand_total - WIN, 0, jnp.where(index < grand_total - SHIFT, 1, 2)
    ).astype(jnp.int32)


def window_place(pos):
    return pos // 32 * SHIFT + pos // SHIFT % SHIFT, pos // 16 % 2 * SHIFT + pos % SHIFT


def parts_of(value):
    high = value.astype(BF16)
    rest = value - high.astype(F32)
    mid = rest.astype(BF16)
    return jnp.concatenate([high, mid, (rest - mid.astype(F32)).astype(BF16)], 0)


def thirds(value):
    rows = value.shape[0] // 3
    return value[:rows] + value[rows : 2 * rows] + value[2 * rows :]


def kernel(
    sizes,
    tok_ref, cot_ref, gain_ref, wq_ref, wp_ref, table_ref, mask_ref,
    mixed_ref, tg_ref, pg_ref, ts_ref,
    xhat, rstd, gath, tile_q, tile_g, back_a, back_d, probs, terms, recv, wsend, wrecv, tsend, trecv, tsum, onehot, bias, flat,
    ag_send, ag_recv, in_send, in_recv, out_send, out_recv, rs_send, rs_recv,
    pl_send, pl_recv,
):
    n, nr, nc, plane, direct, ncol, pg_scale = sizes
    h = lax.axis_index("head")
    r = lax.axis_index("row")
    c = lax.axis_index("col")
    part, width = tok_ref.shape
    group = wp_ref.shape[0]
    ucols = part // UNIT
    COT, NORM = 0, 1

    def at(dr, dc):
        return {"row": lax.rem(r + dr % nr, nr), "col": lax.rem(c + dc % nc, nc)}

    barrier = pltpu.get_barrier_semaphore()
    for dr, dc in plane:
        pl.semaphore_signal(barrier, inc=1, device_id=at(dr, dc), device_id_type=MESH)
    for dh in (1, n - 1):
        pl.semaphore_signal(
            barrier, inc=1, device_id={"head": lax.rem(h + dh, n)}, device_id_type=MESH
        )

    unit_at = lax.broadcasted_iota(jnp.int32, (part, part), 0)
    patch_at = lax.broadcasted_iota(jnp.int32, (part, part), 1)
    wanted = unit_at // SHIFT % SHIFT * ncol + unit_at // UNIT * SHIFT + unit_at % SHIFT
    perm = jnp.where(wanted == patch_at, 1.0, 0.0).astype(BF16)

    x = dot(perm, tok_ref[...], NN)
    cen = x - jnp.mean(x, -1, keepdims=True)
    inv = lax.rsqrt(jnp.mean(cen * cen, -1, keepdims=True) + EPS)
    std = cen * inv
    xhat[...] = std
    rstd[...] = inv
    gath[NORM, h] = (std * gain_ref[...]).astype(BF16)
    gath[COT, h] = dot(perm, cot_ref[...], NN).astype(BF16)
    pl.semaphore_wait(barrier, len(plane) + 2)

    def ag_copy(arr, way, t, blk):
        step = 1 - 2 * way
        return pltpu.make_async_remote_copy(
            src_ref=gath.at[arr, blk], dst_ref=gath.at[arr, blk],
            send_sem=ag_send.at[arr, way, t], recv_sem=ag_recv.at[arr, way, t],
            device_id={"head": h + step}, device_id_type=MESH,
        )

    def sends(way, t):
        if way == 0:
            return (h < n - 1) & (h >= t)
        return (h > 0) & (h < n - t)

    short = jnp.minimum(h, n - 1 - h)

    def arrival(k):
        paired = k <= 2 * short
        way = jnp.where(paired, lax.rem(k - 1, 2), jnp.where(2 * h > n - 1, 0, 1))
        t = jnp.where(paired, (k - 1) // 2, k - 1 - short)
        return way, t, 1 - 2 * way

    def arrived_block(k):
        way, t, step = arrival(k)
        return jnp.where(k == 0, h, h - step * (t + 1))

    def can_send(way):
        return jnp.where(way == 0, h < n - 1, h > 0)

    def receive(arr, k):
        way, t, step = arrival(k)
        blk = h - step * (t + 1)
        pltpu.make_async_remote_copy(
            src_ref=gath.at[arr, blk], dst_ref=gath.at[arr, blk],
            send_sem=ag_send.at[arr, way, t], recv_sem=ag_recv.at[arr, way, t],
            device_id={"head": h - step}, device_id_type=MESH,
        ).wait_recv()

        @pl.when(can_send(way))
        def _():
            ag_copy(arr, way, t + 1, blk).start()

        if arr == NORM:
            last = t + 1 == jnp.where(way == 0, h, n - 1 - h)

            @pl.when(last & can_send(way))
            def _():
                ag_copy(COT, way, 0, h).start()

    def in_copy(kind, k):
        tile = (tile_q, tile_g)[kind]
        if k == 0:
            src, dst, dev = tile.at[0, pl.ds(1, ucols - 1)], tile.at[n, pl.ds(1, ucols - 1)], at(-1, 0)
        elif k == n:
            src, dst, dev = tile.at[0, 0], tile.at[n, ucols], at(-1, -1)
        else:
            src, dst, dev = tile.at[k, 0], tile.at[k, ucols], at(0, -1)
        return pltpu.make_async_remote_copy(
            src_ref=src, dst_ref=dst, send_sem=in_send.at[kind, k], recv_sem=in_recv.at[kind, k],
            device_id=dev, device_id_type=MESH,
        )

    def project(kind, blk):
        if kind == 0:
            for s in range(3):
                out = dot(gath[NORM, blk], wq_ref[s], NN).astype(BF16)
                tile_q[blk, pl.ds(0, ucols), :, pl.ds(s * group, group)] = out.reshape(
                    ucols, UNIT, group
                )
        else:
            out = dot(gath[COT, blk], wp_ref[...], NT).astype(BF16)
            tile_g[blk, pl.ds(0, ucols)] = out.reshape(ucols, UNIT, group)
        for k in range(n):
            @pl.when(blk == k)
            def _():
                in_copy(kind, k).start()
                if k == 0:
                    in_copy(kind, n).start()

    for way in range(2):
        @pl.when(sends(way, 0))
        def _():
            ag_copy(NORM, way, 0, h).start()

        @pl.when(h == (0, n - 1)[way])
        def _():
            ag_copy(COT, way, 0, h).start()

    heads = group // HD
    span = 2 * WIN - 1
    chunk = onehot.shape[2]
    queries = chunk // (2 * HD)
    rows, ids = table_ref.shape

    @pl.loop(0, onehot.shape[0])
    def _(j):
        at_col = lax.broadcasted_iota(jnp.int32, (1, chunk), 1)
        q_at = j * queries + at_col // (2 * HD)
        k_at = at_col % HD
        qr, qc = window_place(q_at)
        kr, kc = window_place(k_at)
        index = (qr - kr + WIN - 1) * span + qc - kc + WIN - 1
        hot = lax.broadcasted_iota(jnp.int32, (ids, chunk), 0) == index
        onehot[j] = jnp.where(hot, 1.0, 0.0).astype(BF16)
        out = thirds(dot(parts_of(table_ref[...]), onehot[j], NN))
        for k in range(heads):
            for q in range(queries):
                bias[k, pl.ds(j * queries + q, 1), :] = out[k : k + 1, q * 2 * HD : (q + 1) * 2 * HD]

    @pl.loop(0, n)
    def _(k):
        @pl.when(k > 0)
        def _():
            receive(NORM, k)

        project(0, arrived_block(k))

    for k in range(n + 1):
        in_copy(0, k).wait_recv()

    lane = lax.broadcasted_iota(jnp.int32, (2 * WIN * WIN, 2 * HD), 1)
    first = lane < HD
    keep0 = jnp.where(first, 1.0, 0.0).astype(BF16)
    keep1 = jnp.where(first, 0.0, 1.0).astype(BF16)
    half = 2 * WIN * WIN
    scale = HD ** (-0.5)
    heads2 = group // (2 * HD)
    pairs2 = ucols // 4

    def places(i, jp):
        return [(2 * i + 1 + ur, 4 * jp + 1 + 2 * w) for w in range(2) for ur in range(2)]

    def load(tile, i, jp, at_lane):
        return jnp.concatenate(
            [
                tile[ur, pl.ds(uc, 2), :, pl.ds(at_lane, 2 * HD)].reshape(2 * UNIT, 2 * HD)
                for ur, uc in places(i, jp)
            ],
            0,
        )

    def save(tile, i, jp, at_lane, value):
        for k, (ur, uc) in enumerate(places(i, jp)):
            tile[ur, pl.ds(uc, 2), :, pl.ds(at_lane, 2 * HD)] = (
                value[2 * UNIT * k : 2 * UNIT * (k + 1)].astype(BF16).reshape(2, UNIT, 2 * HD)
            )

    def both(value):
        return jnp.concatenate([value * keep0, value * keep1], 0)

    def chosen(value):
        return jnp.where(first, value[:half], value[half:])

    def forward(i, jp):
        for hp in range(heads2):
            base = hp * 2 * HD
            q, k, v = [load(tile_q, i, jp, base + s * group) for s in range(3)]
            m = mask_ref[pairs2 * i + jp]
            b = [bias[2 * hp], bias[2 * hp], bias[2 * hp + 1], bias[2 * hp + 1]]
            s = dot(both(q), k, NT) * scale + jnp.concatenate(b, 0) + jnp.concatenate([m, m], 0)
            e = jnp.exp(s - jnp.max(s, -1, keepdims=True))
            p = e / jnp.sum(e, -1, keepdims=True)
            probs[pairs2 * i + jp, hp] = p
            save(back_a, i, jp, base, chosen(dot(p.astype(BF16), v, NN)))

    def backward(i, jp):
        for hp in range(heads2):
            base = hp * 2 * HD
            q, k, v = [load(tile_q, i, jp, base + s * group) for s in range(3)]
            dos = both(load(tile_g, i, jp, base))
            p = probs[pairs2 * i + jp, hp]
            dp = dot(dos, v, NT)
            save(back_d, i, jp, base + 2 * group, dot(p.astype(BF16), dos, TN))
            ds = p * (dp - jnp.sum(p * dp, -1, keepdims=True))
            dsb = ds.astype(BF16)
            save(back_d, i, jp, base, chosen(dot(dsb, k, NN) * scale))
            save(back_d, i, jp, base + group, dot(dsb, both(q), TN) * scale)
            tsum[hp] += ds

    def out_copy(kind, k):
        back = (back_a, back_d)[kind]
        if k == 0:
            src, dst, dev = back.at[n, pl.ds(1, ucols - 1)], back.at[0, pl.ds(1, ucols - 1)], at(1, 0)
        elif k == n:
            src, dst, dev = back.at[n, ucols], back.at[0, 0], at(1, 1)
        else:
            src, dst, dev = back.at[k, ucols], back.at[k, 0], at(0, 1)
        return pltpu.make_async_remote_copy(
            src_ref=src, dst_ref=dst, send_sem=out_send.at[kind, k], recv_sem=out_recv.at[kind, k],
            device_id=dev, device_id_type=MESH,
        )

    def windows(kind, step, between):
        @pl.loop(0, n // 2 * pairs2)
        def _(count):
            i = n // 2 - 1 - count // pairs2
            jp = pairs2 - 1 - lax.rem(count, pairs2)
            step(i, jp)
            for i_at in range(n // 2):
                @pl.when((i == i_at) & (jp == pairs2 - 1))
                def _():
                    out_copy(kind, 2 * i_at + 1).start()
                    out_copy(kind, 2 * i_at + 2).start()

            @pl.when((i == n // 2 - 1) & (jp == 0))
            def _():
                out_copy(kind, 0).start()

            between(count)

    def between_forward(count):
        @pl.when(count < n - 2)
        def _():
            receive(COT, count + 1)

    windows(0, forward, between_forward)
    for k in range(n + 1):
        out_copy(0, k).wait_recv()

    def block(back, d):
        return back[d, pl.ds(0, ucols)].reshape(part, back.shape[-1])

    def rs_copy(arr, way, d):
        step = 1 - 2 * way
        return pltpu.make_async_remote_copy(
            src_ref=terms.at[arr, d], dst_ref=recv.at[arr, way, d],
            send_sem=rs_send.at[arr, way, d], recv_sem=rs_recv.at[arr, way, d],
            device_id={"head": h + step}, device_id_type=MESH,
        )

    def rs_arrived(arr, way, d):
        step = 1 - 2 * way
        pltpu.make_async_remote_copy(
            src_ref=terms.at[arr, d], dst_ref=recv.at[arr, way, d],
            send_sem=rs_send.at[arr, way, d], recv_sem=rs_recv.at[arr, way, d],
            device_id={"head": h - step}, device_id_type=MESH,
        ).wait_recv()

    def order(k):
        far = n - 1 - k // 2
        near = k // 2
        return jnp.where((lax.rem(k, 2) == 0) == (2 * h < n - 1), far, near)

    def rs_start(arr):
        @pl.loop(0, n)
        def _(k):
            d = order(k)
            if arr == 0:
                term = dot(block(back_a, d), wp_ref[...], NN)
            else:
                grads = block(back_d, d)
                term = sum(
                    dot(grads[:, s * group : (s + 1) * group], wq_ref[s], NT) for s in range(3)
                )
            terms[arr, d] = term.astype(BF16)

            @pl.when((h == 0) & (d > 0))
            def _():
                rs_copy(arr, 0, d).start()

            @pl.when((h == n - 1) & (d < n - 1))
            def _():
                rs_copy(arr, 1, d).start()

    def rs_transit(arr, k):
        d = order(k)

        @pl.when(((h < d) & (h > 0)) | ((h > d) & (h < n - 1)))
        def _():
            way = jnp.where(h < d, 0, 1)
            rs_arrived(arr, way, d)
            terms[arr, d] = (terms[arr, d].astype(F32) + recv[arr, way, d].astype(F32)).astype(BF16)
            rs_copy(arr, way, d).start()

    def total(arr):
        sides = [h > 0, h < n - 1]
        for way in range(2):
            @pl.when(sides[way])
            def _():
                rs_arrived(arr, way, h)

            @pl.when(jnp.logical_not(sides[way]))
            def _():
                recv[arr, way, h] = jnp.zeros((part, width), BF16)
        return (
            terms[arr, h].astype(F32) + recv[arr, 0, h].astype(F32) + recv[arr, 1, h].astype(F32)
        )

    rs_start(0)

    @pl.loop(0, n)
    def _(k):
        @pl.when(k == n - 1)
        def _():
            receive(COT, k)

        project(1, arrived_block(k))

    for k in range(n + 1):
        in_copy(1, k).wait_recv()

    tsum[...] = jnp.zeros_like(tsum)
    def between_backward(count):
        @pl.when(count > 0)
        def _():
            rs_transit(0, count - 1)

    windows(1, backward, between_backward)

    for k in range(n + 1):
        out_copy(1, k).wait_recv()
    rs_start(1)

    def pl_copy(kind, o):
        dr, dc = plane[o]
        there = at(dr, dc)
        if kind == 0:
            src, dst = wsend.at[there["row"] * nc + there["col"]], wrecv.at[o]
        else:
            src, dst = tsend, trecv.at[o]
        return pltpu.make_async_remote_copy(
            src_ref=src, dst_ref=dst, send_sem=pl_send.at[kind, o], recv_sem=pl_recv.at[kind, o],
            device_id=there, device_id_type=MESH,
        )

    wide = 2 * 128

    @pl.loop(0, width // wide)
    def _(j):
        attn = back_a[pl.ds(0, n), pl.ds(0, ucols)].reshape(n * part, group)
        cols = pl.ds(pl.multiple_of(j * wide, wide), wide)
        wterm = dot(attn, gath[COT, :, :, cols].reshape(n * part, wide), TN)
        if direct:
            piece = width // (nr * nc)
            for k in range(wide // piece):
                wsend[wide // piece * j + k] = wterm[:, k * piece : (k + 1) * piece].astype(BF16)
        else:
            pg_ref[:, cols] = wterm

    if direct:
        for o in range(len(plane)):
            pl_copy(0, o).start()
    rs_transit(1, 0)

    for k in range(heads):
        hp, at_row = k // 2, k % 2 * half
        bias[k] = tsum[hp, at_row : at_row + HD] + tsum[hp, at_row + HD : at_row + half]
    flat[...] = jnp.zeros_like(flat)
    tsend[...] = jnp.zeros_like(tsend)

    @pl.loop(0, onehot.shape[0])
    def _(j):
        for k in range(heads):
            for q in range(queries):
                flat[k : k + 1, q * 2 * HD : (q + 1) * 2 * HD] = bias[k, pl.ds(j * queries + q, 1), :]
        tsend[...] += thirds(dot(parts_of(flat[...]), onehot[j], NT))

    if direct:
        for o in range(len(plane)):
            pl_copy(1, o).start()
    else:
        ts_ref[...] = tsend[...]

    @pl.loop(1, n - 1)
    def _(k):
        rs_transit(1, k)

    mixed = dot(perm, tok_ref[...], NN) + total(0)
    mixed_ref[...] = dot(perm, mixed.astype(BF16), TN).astype(BF16)

    if direct:
        for o in range(len(plane)):
            for kind in range(2):
                pl_copy(kind, o).wait_recv()
        wsum = wsend[r * nc + c].astype(F32)
        tall = tsend[...]
        for o in range(len(plane)):
            wsum = wsum + wrecv[o].astype(F32)
            tall = tall + trecv[o]
        pg_ref[...] = wsum * pg_scale
        ts_ref[...] = tall
        for o in range(len(plane)):
            for kind in range(2):
                pl_copy(kind, o).wait_send()

    gg = total(1) * gain_ref[...]
    std = xhat[...]
    tg = gath[COT, h].astype(F32) + rstd[...] * (
        gg - jnp.mean(gg, -1, keepdims=True) - std * jnp.mean(gg * std, -1, keepdims=True)
    )
    tg_ref[...] = dot(perm, tg.astype(BF16), TN).astype(BF16)

    for arr in range(2):
        for way in range(2):
            for t in range(n - 1):
                @pl.when(sends(way, t))
                def _():
                    ag_copy(arr, way, t, h - (1 - 2 * way) * t).wait_send()
    for kind in range(2):
        for k in range(n + 1):
            in_copy(kind, k).wait_send()
            out_copy(kind, k).wait_send()
    for arr in range(2):
        for d in range(n):
            if d > 0:
                @pl.when(h < d)
                def _():
                    rs_copy(arr, 0, d).wait_send()
            if d < n - 1:
                @pl.when(h > d)
                def _():
                    rs_copy(arr, 1, d).wait_send()


def on_device(n, nr, nc, tokens, valid, gain, w_qkv, w_proj, rel_table, cotangent):
    part_rows, ncol, width = tokens.shape
    tile_rows = part_rows * n
    part = part_rows * ncol
    heads = rel_table.shape[1]
    group = heads * HD
    pairs = heads // 2
    pos = WIN * WIN
    ucols = ncol // SHIFT

    row_lab = region(
        lax.axis_index("row") * tile_rows + jnp.arange(tile_rows, dtype=jnp.int32), tile_rows * nr
    )
    col_lab = region(lax.axis_index("col") * ncol + jnp.arange(ncol, dtype=jnp.int32), ncol * nc)
    labels = 3 * row_lab[:, None] + col_lab[None, :]

    def to_pairs(block):
        block = block.reshape(tile_rows // WIN, 2, SHIFT, ncol // WIN, 2, SHIFT)
        return block.transpose(0, 3, 1, 4, 2, 5).reshape(-1, 2 * pos)

    lab = to_pairs(labels) + 16 * (jnp.arange(2 * pos, dtype=jnp.int32) // pos)[None]
    val = to_pairs(valid)
    allowed = (lab[:, :, None] == lab[:, None, :]) & (
        (val[:, None, :] == 1) | jnp.eye(2 * pos, dtype=bool)[None]
    )
    mask = jnp.where(allowed, 0.0, -1e30).astype(F32)
    rows, ids = -(-heads // 16) * 16, 256
    table = jnp.pad(rel_table.T, ((0, rows - heads), (0, ids - rel_table.shape[0])))
    scale = 1.0 / math.sqrt(tile_rows * ncol * nr * nc)
    direct = nr * nc <= 8
    if direct:
        plane = [(dr, dc) for dr in range(nr) for dc in range(nc) if (dr, dc) != (0, 0)]
    else:
        six = [(1, 0), (nr - 1, 0), (0, 1), (0, nc - 1), (1, 1), (nr - 1, nc - 1)]
        plane = sorted(set(six))
    count = len(plane)
    piece = width // (nr * nc)
    vmem = pl.BlockSpec(memory_space=pltpu.VMEM)
    dma = pltpu.SemaphoreType.DMA
    mixed, token_gradient, wsum, tall = pl.pallas_call(
        functools.partial(kernel, (n, nr, nc, tuple(plane), direct, ncol, scale)),
        out_shape=(
            jax.ShapeDtypeStruct((part, width), BF16),
            jax.ShapeDtypeStruct((part, width), BF16),
            jax.ShapeDtypeStruct((group, piece if direct else width), F32),
            jax.ShapeDtypeStruct((rows, ids), F32),
        ),
        in_specs=[vmem] * 7,
        out_specs=[vmem] * 4,
        scratch_shapes=[
            pltpu.VMEM((part, width), F32),
            pltpu.VMEM((part, 1), F32),
            pltpu.VMEM((2, n, part, width), BF16),
            pltpu.VMEM((n + 1, ucols + 1, UNIT, 3 * group), BF16),
            pltpu.VMEM((n + 1, ucols + 1, UNIT, group), BF16),
            pltpu.VMEM((n + 1, ucols + 1, UNIT, group), BF16),
            pltpu.VMEM((n + 1, ucols + 1, UNIT, 3 * group), BF16),
            pltpu.VMEM((n * ucols // 8, pairs, 4 * pos, 2 * pos), F32),
            pltpu.VMEM((2, n, part, width), BF16),
            pltpu.VMEM((2, 2, n, part, width), BF16),
            pltpu.VMEM((nr * nc, group, piece) if direct else (1, 16, 128), BF16),
            pltpu.VMEM((count, group, piece) if direct else (1, 16, 128), BF16),
            pltpu.VMEM((rows, ids), F32),
            pltpu.VMEM((count, rows, ids) if direct else (1, 16, 128), F32),
            pltpu.VMEM((pairs, 4 * pos, 2 * pos), F32),
            pltpu.VMEM((pos // 4, ids, 8 * HD), BF16),
            pltpu.VMEM((heads, pos, 2 * HD), F32),
            pltpu.VMEM((rows, 8 * HD), F32),
            dma((2, 2, n)),
            dma((2, 2, n)),
            dma((2, n + 1)),
            dma((2, n + 1)),
            dma((2, n + 1)),
            dma((2, n + 1)),
            dma((2, 2, n)),
            dma((2, 2, n)),
            dma((2, count)),
            dma((2, count)),
        ],
        compiler_params=pltpu.CompilerParams(
            collective_id=0, has_side_effects=True, vmem_limit_bytes=48 * 1024 * 1024
        ),
    )(
        tokens.reshape(part, width),
        cotangent.reshape(part, width),
        gain[None],
        w_qkv.transpose(1, 0, 2),
        w_proj,
        table,
        mask,
    )
    if not direct:
        wsum = lax.psum_scatter(wsum, ("row", "col"), scatter_dimension=1, tiled=True) * scale
        tall = lax.psum(tall, ("row", "col"))
    table_grad = tall[:heads, : rel_table.shape[0]].T * (WIN * scale)
    return (
        mixed.reshape(part_rows, ncol, width),
        token_gradient.reshape(part_rows, ncol, width),
        wsum,
        table_grad,
    )


def solution(mesh):
    n, nr, nc = (mesh.shape[name] for name in ("head", "row", "col"))
    return jax.shard_map(
        functools.partial(on_device, n, nr, nc),
        mesh=mesh,
        in_specs=(
            P(("row", "head"), "col", None),
            P("row", "col"),
            P(),
            P(None, None, "head"),
            P("head", None),
            P(None, "head"),
            P(("row", "head"), "col", None),
        ),
        out_specs=(
            P(("row", "head"), "col", None),
            P(("row", "head"), "col", None),
            P("head", ("row", "col")),
            P(None, "head"),
        ),
        check_vma=False,
    )
```

```python
import functools
import math

import jax
import jax.numpy as jnp
from jax import lax
from jax.experimental import pallas as pl
from jax.experimental.pallas import tpu as pltpu
from jax.sharding import PartitionSpec as P

HD = 64
WIN = 8
SHIFT = 4
UNIT = SHIFT * SHIFT
EPS = 1e-05
MESH = pl.DeviceIdType.MESH
F32 = jnp.float32
BF16 = jnp.bfloat16
NN = (((1,), (0,)), ((), ()))
NT = (((1,), (1,)), ((), ()))
TN = (((0,), (0,)), ((), ()))


def dot(a, b, dims):
    return lax.dot_general(a, b, dims, preferred_element_type=F32)


def region(index, grand_total):
    return jnp.where(
        index < grand_total - WIN, 0, jnp.where(index < grand_total - SHIFT, 1, 2)
    ).astype(jnp.int32)


def window_place(pos):
    return pos // 32 * SHIFT + pos // SHIFT % SHIFT, pos // 16 % 2 * SHIFT + pos % SHIFT


def parts_of(value):
    high = value.astype(BF16)
    rest = value - high.astype(F32)
    mid = rest.astype(BF16)
    return jnp.concatenate([high, mid, (rest - mid.astype(F32)).astype(BF16)], 0)


def thirds(value):
    rows = value.shape[0] // 3
    return value[:rows] + value[rows : 2 * rows] + value[2 * rows :]


def kernel(
    sizes,
    tok_hbm, cot_hbm, gain_ref, wq_hbm, wp_hbm, table_ref, valid_ref,
    mixed_ref, tg_ref, pg_ref, ts_ref,
    xhat, rstd, gath, tile_q, tile_g, back_a, back_d, probs, terms, recv, wsend, wrecv, tsend, trecv, tsum, onehot, bias, flat,
    tok_ref, cot_ref, wq_ref, wp_ref, load_sem,
    ag_send, ag_recv, in_send, in_recv, out_send, out_recv, rs_send, rs_recv,
    pl_send, pl_recv,
):
    n, nr, nc, plane, direct, ncol, pg_scale = sizes
    h = lax.axis_index("head")
    r = lax.axis_index("row")
    c = lax.axis_index("col")
    part, width = tok_ref.shape
    group = wp_ref.shape[0]
    ucols = part // UNIT
    COT, NORM = 0, 1

    def at(dr, dc):
        return {"row": lax.rem(r + dr % nr, nr), "col": lax.rem(c + dc % nc, nc)}

    sources = (tok_hbm, cot_hbm, wq_hbm, wp_hbm)
    targets = (tok_ref, cot_ref, wq_ref, wp_ref)
    loads = [
        pltpu.make_async_copy(src, dst, load_sem.at[k])
        for k, (src, dst) in enumerate(zip(sources, targets))
    ]
    for copy in loads:
        copy.start()
    barrier = pltpu.get_barrier_semaphore()
    for dr, dc in plane:
        pl.semaphore_signal(barrier, inc=1, device_id=at(dr, dc), device_id_type=MESH)
    for dh in (1, n - 1):
        pl.semaphore_signal(
            barrier, inc=1, device_id={"head": lax.rem(h + dh, n)}, device_id_type=MESH
        )

    unit_at = lax.broadcasted_iota(jnp.int32, (part, part), 0)
    patch_at = lax.broadcasted_iota(jnp.int32, (part, part), 1)
    wanted = unit_at // SHIFT % SHIFT * ncol + unit_at // UNIT * SHIFT + unit_at % SHIFT
    perm = jnp.where(wanted == patch_at, 1.0, 0.0).astype(BF16)

    loads[0].wait()
    x = dot(perm, tok_ref[...], NN)
    cen = x - jnp.mean(x, -1, keepdims=True)
    inv = lax.rsqrt(jnp.mean(cen * cen, -1, keepdims=True) + EPS)
    std = cen * inv
    xhat[...] = std
    rstd[...] = inv
    gath[NORM, h] = (std * gain_ref[...]).astype(BF16)
    loads[1].wait()
    gath[COT, h] = dot(perm, cot_ref[...], NN).astype(BF16)
    pl.semaphore_wait(barrier, len(plane) + 2)

    def ag_copy(arr, way, t, blk):
        step = 1 - 2 * way
        return pltpu.make_async_remote_copy(
            src_ref=gath.at[arr, blk], dst_ref=gath.at[arr, blk],
            send_sem=ag_send.at[arr, way, t], recv_sem=ag_recv.at[arr, way, t],
            device_id={"head": h + step}, device_id_type=MESH,
        )

    def sends(way, t):
        if way == 0:
            return (h < n - 1) & (h >= t)
        return (h > 0) & (h < n - t)

    short = jnp.minimum(h, n - 1 - h)

    def arrival(k):
        paired = k <= 2 * short
        way = jnp.where(paired, lax.rem(k - 1, 2), jnp.where(2 * h > n - 1, 0, 1))
        t = jnp.where(paired, (k - 1) // 2, k - 1 - short)
        return way, t, 1 - 2 * way

    def arrived_block(k):
        way, t, step = arrival(k)
        return jnp.where(k == 0, h, h - step * (t + 1))

    def can_send(way):
        return jnp.where(way == 0, h < n - 1, h > 0)

    def receive(arr, k):
        way, t, step = arrival(k)
        blk = h - step * (t + 1)
        pltpu.make_async_remote_copy(
            src_ref=gath.at[arr, blk], dst_ref=gath.at[arr, blk],
            send_sem=ag_send.at[arr, way, t], recv_sem=ag_recv.at[arr, way, t],
            device_id={"head": h - step}, device_id_type=MESH,
        ).wait_recv()

        @pl.when(can_send(way))
        def _():
            ag_copy(arr, way, t + 1, blk).start()

        if arr == NORM:
            last = t + 1 == jnp.where(way == 0, h, n - 1 - h)

            @pl.when(last & can_send(way))
            def _():
                ag_copy(COT, way, 0, h).start()

    def in_copy(kind, k):
        tile = (tile_q, tile_g)[kind]
        if k == 0:
            src, dst, dev = tile.at[0, pl.ds(1, ucols - 1)], tile.at[n, pl.ds(1, ucols - 1)], at(-1, 0)
        elif k == n:
            src, dst, dev = tile.at[0, 0], tile.at[n, ucols], at(-1, -1)
        else:
            src, dst, dev = tile.at[k, 0], tile.at[k, ucols], at(0, -1)
        return pltpu.make_async_remote_copy(
            src_ref=src, dst_ref=dst, send_sem=in_send.at[kind, k], recv_sem=in_recv.at[kind, k],
            device_id=dev, device_id_type=MESH,
        )

    def project(kind, blk):
        if kind == 0:
            for s in range(3):
                out = dot(gath[NORM, blk], wq_ref[s], NN).astype(BF16)
                tile_q[blk, pl.ds(0, ucols), :, pl.ds(s * group, group)] = out.reshape(
                    ucols, UNIT, group
                )
        else:
            out = dot(gath[COT, blk], wp_ref[...], NT).astype(BF16)
            tile_g[blk, pl.ds(0, ucols)] = out.reshape(ucols, UNIT, group)
        for k in range(n):
            @pl.when(blk == k)
            def _():
                in_copy(kind, k).start()
                if k == 0:
                    in_copy(kind, n).start()

    for way in range(2):
        @pl.when(sends(way, 0))
        def _():
            ag_copy(NORM, way, 0, h).start()

        @pl.when(h == (0, n - 1)[way])
        def _():
            ag_copy(COT, way, 0, h).start()

    heads = group // HD
    span = 2 * WIN - 1
    chunk = onehot.shape[2]
    queries = chunk // (2 * HD)
    rows, ids = table_ref.shape

    @pl.loop(0, onehot.shape[0])
    def _(j):
        at_col = lax.broadcasted_iota(jnp.int32, (1, chunk), 1)
        q_at = j * queries + at_col // (2 * HD)
        k_at = at_col % HD
        qr, qc = window_place(q_at)
        kr, kc = window_place(k_at)
        index = (qr - kr + WIN - 1) * span + qc - kc + WIN - 1
        hot = lax.broadcasted_iota(jnp.int32, (ids, chunk), 0) == index
        onehot[j] = jnp.where(hot, 1.0, 0.0).astype(BF16)
        out = thirds(dot(parts_of(table_ref[...]), onehot[j], NN))
        for k in range(heads):
            for q in range(queries):
                bias[k, pl.ds(j * queries + q, 1), :] = out[k : k + 1, q * 2 * HD : (q + 1) * 2 * HD]

    loads[2].wait()
    loads[3].wait()

    @pl.loop(0, n)
    def _(k):
        @pl.when(k > 0)
        def _():
            receive(NORM, k)

        project(0, arrived_block(k))

    for k in range(n + 1):
        in_copy(0, k).wait_recv()

    lane = lax.broadcasted_iota(jnp.int32, (2 * WIN * WIN, 2 * HD), 1)
    first = lane < HD
    keep0 = jnp.where(first, 1.0, 0.0).astype(BF16)
    keep1 = jnp.where(first, 0.0, 1.0).astype(BF16)
    half = 2 * WIN * WIN
    scale = HD ** (-0.5)
    heads2 = group // (2 * HD)
    pairs2 = ucols // 4

    def places(i, jp):
        return [(2 * i + 1 + ur, 4 * jp + 1 + 2 * w) for w in range(2) for ur in range(2)]

    def load(tile, i, jp, at_lane):
        return jnp.concatenate(
            [
                tile[ur, pl.ds(uc, 2), :, pl.ds(at_lane, 2 * HD)].reshape(2 * UNIT, 2 * HD)
                for ur, uc in places(i, jp)
            ],
            0,
        )

    def save(tile, i, jp, at_lane, value):
        for k, (ur, uc) in enumerate(places(i, jp)):
            tile[ur, pl.ds(uc, 2), :, pl.ds(at_lane, 2 * HD)] = (
                value[2 * UNIT * k : 2 * UNIT * (k + 1)].astype(BF16).reshape(2, UNIT, 2 * HD)
            )

    def both(value):
        return jnp.concatenate([value * keep0, value * keep1], 0)

    def chosen(value):
        return jnp.where(first, value[:half], value[half:])

    def labels(i, jp, pos):
        window = pos // (WIN * WIN)
        prow, pcol = window_place(pos % (WIN * WIN))
        row = region((r * (n // 2) + i) * WIN + prow, nr * n * SHIFT)
        col = region(c * ncol + (2 * jp + window) * WIN + pcol, nc * ncol)
        return 16 * window + 3 * row + col

    def mask_of(i, jp):
        q_at = lax.broadcasted_iota(jnp.int32, (half, 1), 0)
        k_at = lax.broadcasted_iota(jnp.int32, (1, half), 1)
        same = labels(i, jp, q_at) == labels(i, jp, k_at)
        kept = (valid_ref[pl.ds(pairs2 * i + jp, 1), :] == 1) | (q_at == k_at)
        return jnp.where(same & kept, 0.0, -1e30)

    def forward(i, jp):
        m = mask_of(i, jp)
        for hp in range(heads2):
            base = hp * 2 * HD
            q, k, v = [load(tile_q, i, jp, base + s * group) for s in range(3)]
            b = [bias[2 * hp], bias[2 * hp], bias[2 * hp + 1], bias[2 * hp + 1]]
            s = dot(both(q), k, NT) * scale + jnp.concatenate(b, 0) + jnp.concatenate([m, m], 0)
            e = jnp.exp(s - jnp.max(s, -1, keepdims=True))
            p = e / jnp.sum(e, -1, keepdims=True)
            probs[pairs2 * i + jp, hp] = p
            save(back_a, i, jp, base, chosen(dot(p.astype(BF16), v, NN)))

    def backward(i, jp):
        for hp in range(heads2):
            base = hp * 2 * HD
            q, k, v = [load(tile_q, i, jp, base + s * group) for s in range(3)]
            dos = both(load(tile_g, i, jp, base))
            p = probs[pairs2 * i + jp, hp]
            dp = dot(dos, v, NT)
            save(back_d, i, jp, base + 2 * group, dot(p.astype(BF16), dos, TN))
            ds = p * (dp - jnp.sum(p * dp, -1, keepdims=True))
            dsb = ds.astype(BF16)
            save(back_d, i, jp, base, chosen(dot(dsb, k, NN) * scale))
            save(back_d, i, jp, base + group, dot(dsb, both(q), TN) * scale)
            tsum[hp] += ds

    def out_copy(kind, k):
        back = (back_a, back_d)[kind]
        if k == 0:
            src, dst, dev = back.at[n, pl.ds(1, ucols - 1)], back.at[0, pl.ds(1, ucols - 1)], at(1, 0)
        elif k == n:
            src, dst, dev = back.at[n, ucols], back.at[0, 0], at(1, 1)
        else:
            src, dst, dev = back.at[k, ucols], back.at[k, 0], at(0, 1)
        return pltpu.make_async_remote_copy(
            src_ref=src, dst_ref=dst, send_sem=out_send.at[kind, k], recv_sem=out_recv.at[kind, k],
            device_id=dev, device_id_type=MESH,
        )

    def windows(kind, step, between):
        @pl.loop(0, n // 2 * pairs2)
        def _(count):
            i = n // 2 - 1 - count // pairs2
            jp = pairs2 - 1 - lax.rem(count, pairs2)
            step(i, jp)
            for i_at in range(n // 2):
                @pl.when((i == i_at) & (jp == pairs2 - 1))
                def _():
                    out_copy(kind, 2 * i_at + 1).start()
                    out_copy(kind, 2 * i_at + 2).start()

            @pl.when((i == n // 2 - 1) & (jp == 0))
            def _():
                out_copy(kind, 0).start()

            between(count)

    def between_forward(count):
        @pl.when(count < n - 2)
        def _():
            receive(COT, count + 1)

    windows(0, forward, between_forward)
    for k in range(n + 1):
        out_copy(0, k).wait_recv()

    def block(back, d):
        return back[d, pl.ds(0, ucols)].reshape(part, back.shape[-1])

    def rs_copy(arr, way, d):
        step = 1 - 2 * way
        return pltpu.make_async_remote_copy(
            src_ref=terms.at[arr, d], dst_ref=recv.at[arr, way, d],
            send_sem=rs_send.at[arr, way, d], recv_sem=rs_recv.at[arr, way, d],
            device_id={"head": h + step}, device_id_type=MESH,
        )

    def rs_arrived(arr, way, d):
        step = 1 - 2 * way
        pltpu.make_async_remote_copy(
            src_ref=terms.at[arr, d], dst_ref=recv.at[arr, way, d],
            send_sem=rs_send.at[arr, way, d], recv_sem=rs_recv.at[arr, way, d],
            device_id={"head": h - step}, device_id_type=MESH,
        ).wait_recv()

    def order(k):
        far = n - 1 - k // 2
        near = k // 2
        return jnp.where((lax.rem(k, 2) == 0) == (2 * h < n - 1), far, near)

    def rs_start(arr):
        @pl.loop(0, n)
        def _(k):
            d = order(k)
            if arr == 0:
                term = dot(block(back_a, d), wp_ref[...], NN)
            else:
                grads = block(back_d, d)
                term = sum(
                    dot(grads[:, s * group : (s + 1) * group], wq_ref[s], NT) for s in range(3)
                )
            terms[arr, d] = term.astype(BF16)

            @pl.when((h == 0) & (d > 0))
            def _():
                rs_copy(arr, 0, d).start()

            @pl.when((h == n - 1) & (d < n - 1))
            def _():
                rs_copy(arr, 1, d).start()

    def rs_transit(arr, k):
        d = order(k)

        @pl.when(((h < d) & (h > 0)) | ((h > d) & (h < n - 1)))
        def _():
            way = jnp.where(h < d, 0, 1)
            rs_arrived(arr, way, d)
            terms[arr, d] = (terms[arr, d].astype(F32) + recv[arr, way, d].astype(F32)).astype(BF16)
            rs_copy(arr, way, d).start()

    def total(arr):
        sides = [h > 0, h < n - 1]
        for way in range(2):
            @pl.when(sides[way])
            def _():
                rs_arrived(arr, way, h)

            @pl.when(jnp.logical_not(sides[way]))
            def _():
                recv[arr, way, h] = jnp.zeros((part, width), BF16)
        return (
            terms[arr, h].astype(F32) + recv[arr, 0, h].astype(F32) + recv[arr, 1, h].astype(F32)
        )

    rs_start(0)

    @pl.loop(0, n)
    def _(k):
        @pl.when(k == n - 1)
        def _():
            receive(COT, k)

        project(1, arrived_block(k))

    for k in range(n + 1):
        in_copy(1, k).wait_recv()

    tsum[...] = jnp.zeros_like(tsum)
    def between_backward(count):
        @pl.when(count > 0)
        def _():
            rs_transit(0, count - 1)

    windows(1, backward, between_backward)

    for k in range(n + 1):
        out_copy(1, k).wait_recv()
    rs_start(1)

    def pl_copy(kind, o):
        dr, dc = plane[o]
        there = at(dr, dc)
        if kind == 0:
            src, dst = wsend.at[there["row"] * nc + there["col"]], wrecv.at[o]
        else:
            src, dst = tsend, trecv.at[o]
        return pltpu.make_async_remote_copy(
            src_ref=src, dst_ref=dst, send_sem=pl_send.at[kind, o], recv_sem=pl_recv.at[kind, o],
            device_id=there, device_id_type=MESH,
        )

    wide = 2 * 128

    @pl.loop(0, width // wide)
    def _(j):
        attn = back_a[pl.ds(0, n), pl.ds(0, ucols)].reshape(n * part, group)
        cols = pl.ds(pl.multiple_of(j * wide, wide), wide)
        wterm = dot(attn, gath[COT, :, :, cols].reshape(n * part, wide), TN)
        if direct:
            piece = width // (nr * nc)
            for k in range(wide // piece):
                wsend[wide // piece * j + k] = wterm[:, k * piece : (k + 1) * piece].astype(BF16)
        else:
            pg_ref[:, cols] = wterm

    if direct:
        for o in range(len(plane)):
            pl_copy(0, o).start()
    rs_transit(1, 0)

    for k in range(heads):
        hp, at_row = k // 2, k % 2 * half
        bias[k] = tsum[hp, at_row : at_row + HD] + tsum[hp, at_row + HD : at_row + half]
    flat[...] = jnp.zeros_like(flat)
    tsend[...] = jnp.zeros_like(tsend)

    @pl.loop(0, onehot.shape[0])
    def _(j):
        for k in range(heads):
            for q in range(queries):
                flat[k : k + 1, q * 2 * HD : (q + 1) * 2 * HD] = bias[k, pl.ds(j * queries + q, 1), :]
        tsend[...] += thirds(dot(parts_of(flat[...]), onehot[j], NT))

    if direct:
        for o in range(len(plane)):
            pl_copy(1, o).start()
    else:
        ts_ref[...] = tsend[...]

    @pl.loop(1, n - 1)
    def _(k):
        rs_transit(1, k)

    mixed = dot(perm, tok_ref[...], NN) + total(0)
    mixed_ref[...] = dot(perm, mixed.astype(BF16), TN).astype(BF16)

    if direct:
        for o in range(len(plane)):
            for kind in range(2):
                pl_copy(kind, o).wait_recv()
        wsum = wsend[r * nc + c].astype(F32)
        tall = tsend[...]
        for o in range(len(plane)):
            wsum = wsum + wrecv[o].astype(F32)
            tall = tall + trecv[o]
        pg_ref[...] = wsum * pg_scale
        ts_ref[...] = tall
        for o in range(len(plane)):
            for kind in range(2):
                pl_copy(kind, o).wait_send()

    gg = total(1) * gain_ref[...]
    std = xhat[...]
    tg = gath[COT, h].astype(F32) + rstd[...] * (
        gg - jnp.mean(gg, -1, keepdims=True) - std * jnp.mean(gg * std, -1, keepdims=True)
    )
    tg_ref[...] = dot(perm, tg.astype(BF16), TN).astype(BF16)

    for arr in range(2):
        for way in range(2):
            for t in range(n - 1):
                @pl.when(sends(way, t))
                def _():
                    ag_copy(arr, way, t, h - (1 - 2 * way) * t).wait_send()
    for kind in range(2):
        for k in range(n + 1):
            in_copy(kind, k).wait_send()
            out_copy(kind, k).wait_send()
    for arr in range(2):
        for d in range(n):
            if d > 0:
                @pl.when(h < d)
                def _():
                    rs_copy(arr, 0, d).wait_send()
            if d < n - 1:
                @pl.when(h > d)
                def _():
                    rs_copy(arr, 1, d).wait_send()


def on_device(n, nr, nc, tokens, valid, gain, w_qkv, w_proj, rel_table, cotangent):
    part_rows, ncol, width = tokens.shape
    tile_rows = part_rows * n
    part = part_rows * ncol
    heads = rel_table.shape[1]
    group = heads * HD
    pairs = heads // 2
    pos = WIN * WIN
    ucols = ncol // SHIFT

    def to_pairs(block):
        block = block.reshape(tile_rows // WIN, 2, SHIFT, ncol // WIN, 2, SHIFT)
        return block.transpose(0, 3, 1, 4, 2, 5).reshape(-1, 2 * pos)

    rows, ids = -(-heads // 16) * 16, 256
    table = jnp.pad(rel_table.T, ((0, rows - heads), (0, ids - rel_table.shape[0])))
    scale = 1.0 / math.sqrt(tile_rows * ncol * nr * nc)
    direct = nr * nc <= 8
    if direct:
        plane = [(dr, dc) for dr in range(nr) for dc in range(nc) if (dr, dc) != (0, 0)]
    else:
        six = [(1, 0), (nr - 1, 0), (0, 1), (0, nc - 1), (1, 1), (nr - 1, nc - 1)]
        plane = sorted(set(six))
    count = len(plane)
    piece = width // (nr * nc)
    vmem = pl.BlockSpec(memory_space=pltpu.VMEM)
    hbm = pl.BlockSpec(memory_space=pltpu.HBM)
    dma = pltpu.SemaphoreType.DMA
    mixed, token_gradient, wsum, tall = pl.pallas_call(
        functools.partial(kernel, (n, nr, nc, tuple(plane), direct, ncol, scale)),
        out_shape=(
            jax.ShapeDtypeStruct((part, width), BF16),
            jax.ShapeDtypeStruct((part, width), BF16),
            jax.ShapeDtypeStruct((group, piece if direct else width), F32),
            jax.ShapeDtypeStruct((rows, ids), F32),
        ),
        in_specs=[hbm, hbm, vmem, hbm, hbm, vmem, vmem],
        out_specs=[vmem] * 4,
        scratch_shapes=[
            pltpu.VMEM((part, width), F32),
            pltpu.VMEM((part, 1), F32),
            pltpu.VMEM((2, n, part, width), BF16),
            pltpu.VMEM((n + 1, ucols + 1, UNIT, 3 * group), BF16),
            pltpu.VMEM((n + 1, ucols + 1, UNIT, group), BF16),
            pltpu.VMEM((n + 1, ucols + 1, UNIT, group), BF16),
            pltpu.VMEM((n + 1, ucols + 1, UNIT, 3 * group), BF16),
            pltpu.VMEM((n * ucols // 8, pairs, 4 * pos, 2 * pos), F32),
            pltpu.VMEM((2, n, part, width), BF16),
            pltpu.VMEM((2, 2, n, part, width), BF16),
            pltpu.VMEM((nr * nc, group, piece) if direct else (1, 16, 128), BF16),
            pltpu.VMEM((count, group, piece) if direct else (1, 16, 128), BF16),
            pltpu.VMEM((rows, ids), F32),
            pltpu.VMEM((count, rows, ids) if direct else (1, 16, 128), F32),
            pltpu.VMEM((pairs, 4 * pos, 2 * pos), F32),
            pltpu.VMEM((pos // 4, ids, 8 * HD), BF16),
            pltpu.VMEM((heads, pos, 2 * HD), F32),
            pltpu.VMEM((rows, 8 * HD), F32),
            pltpu.VMEM((part, width), BF16),
            pltpu.VMEM((part, width), BF16),
            pltpu.VMEM((3, width, group), BF16),
            pltpu.VMEM((group, width), BF16),
            dma((4,)),
            dma((2, 2, n)),
            dma((2, 2, n)),
            dma((2, n + 1)),
            dma((2, n + 1)),
            dma((2, n + 1)),
            dma((2, n + 1)),
            dma((2, 2, n)),
            dma((2, 2, n)),
            dma((2, count)),
            dma((2, count)),
        ],
        compiler_params=pltpu.CompilerParams(
            collective_id=0, has_side_effects=True, vmem_limit_bytes=60 * 1024 * 1024
        ),
    )(
        tokens.reshape(part, width),
        cotangent.reshape(part, width),
        gain[None],
        w_qkv.transpose(1, 0, 2),
        w_proj,
        table,
        to_pairs(valid),
    )
    if not direct:
        wsum = lax.psum_scatter(wsum, ("row", "col"), scatter_dimension=1, tiled=True) * scale
        tall = lax.psum(tall, ("row", "col"))
    table_grad = tall[:heads, : rel_table.shape[0]].T * (WIN * scale)
    return (
        mixed.reshape(part_rows, ncol, width),
        token_gradient.reshape(part_rows, ncol, width),
        wsum,
        table_grad,
    )


def solution(mesh):
    n, nr, nc = (mesh.shape[name] for name in ("head", "row", "col"))
    return jax.shard_map(
        functools.partial(on_device, n, nr, nc),
        mesh=mesh,
        in_specs=(
            P(("row", "head"), "col", None),
            P("row", "col"),
            P(),
            P(None, None, "head"),
            P("head", None),
            P(None, "head"),
            P(("row", "head"), "col", None),
        ),
        out_specs=(
            P(("row", "head"), "col", None),
            P(("row", "head"), "col", None),
            P("head", ("row", "col")),
            P(None, "head"),
        ),
        check_vma=False,
    )
```

```python
import functools
import math

import jax
import jax.numpy as jnp
from jax import lax
from jax.experimental import pallas as pl
from jax.experimental.pallas import tpu as pltpu
from jax.sharding import PartitionSpec as P

HD = 64
WIN = 8
SHIFT = 4
UNIT = SHIFT * SHIFT
EPS = 1e-05
MESH = pl.DeviceIdType.MESH
F32 = jnp.float32
BF16 = jnp.bfloat16
NN = (((1,), (0,)), ((), ()))
NT = (((1,), (1,)), ((), ()))
TN = (((0,), (0,)), ((), ()))


def dot(a, b, dims):
    return lax.dot_general(a, b, dims, preferred_element_type=F32)


def region(index, grand_total):
    return jnp.where(
        index < grand_total - WIN, 0, jnp.where(index < grand_total - SHIFT, 1, 2)
    ).astype(jnp.int32)


def window_place(pos):
    return pos // 32 * SHIFT + pos // SHIFT % SHIFT, pos // 16 % 2 * SHIFT + pos % SHIFT


def parts_of(value):
    high = value.astype(BF16)
    rest = value - high.astype(F32)
    mid = rest.astype(BF16)
    return jnp.concatenate([high, mid, (rest - mid.astype(F32)).astype(BF16)], 0)


def thirds(value):
    rows = value.shape[0] // 3
    return value[:rows] + value[rows : 2 * rows] + value[2 * rows :]


def kernel(
    sizes,
    tok_hbm, cot_hbm, gain_ref, wq_hbm, wp_hbm, table_ref, valid_ref,
    mixed_ref, tg_ref, pg_ref, ts_ref,
    xhat, rstd, gath, tile_q, tile_g, back_a, back_d, probs, terms, recv, wsend, wrecv, tsend, trecv, tsum, onehot, bias, flat,
    tok_ref, cot_ref, wq_ref, wp_ref, load_sem,
    ag_send, ag_recv, in_send, in_recv, out_send, out_recv, rs_send, rs_recv,
    pl_send, pl_recv,
):
    n, nr, nc, plane, direct, ncol, pg_scale = sizes
    h = lax.axis_index("head")
    r = lax.axis_index("row")
    c = lax.axis_index("col")
    part, width = tok_ref.shape
    group = wp_ref.shape[0]
    ucols = part // UNIT
    COT, NORM = 0, 1

    def at(dr, dc):
        return {"row": lax.rem(r + dr % nr, nr), "col": lax.rem(c + dc % nc, nc)}

    sources = (tok_hbm, cot_hbm, wq_hbm, wp_hbm)
    targets = (tok_ref, cot_ref, wq_ref, wp_ref)
    loads = [
        pltpu.make_async_copy(src, dst, load_sem.at[k])
        for k, (src, dst) in enumerate(zip(sources, targets))
    ]
    for copy in loads:
        copy.start()
    barrier = pltpu.get_barrier_semaphore()
    for dr, dc in plane:
        pl.semaphore_signal(barrier, inc=1, device_id=at(dr, dc), device_id_type=MESH)
    for dh in (1, n - 1):
        pl.semaphore_signal(
            barrier, inc=1, device_id={"head": lax.rem(h + dh, n)}, device_id_type=MESH
        )

    unit_at = lax.broadcasted_iota(jnp.int32, (part, part), 0)
    patch_at = lax.broadcasted_iota(jnp.int32, (part, part), 1)
    wanted = unit_at // SHIFT % SHIFT * ncol + unit_at // UNIT * SHIFT + unit_at % SHIFT
    perm = jnp.where(wanted == patch_at, 1.0, 0.0).astype(BF16)

    loads[0].wait()
    x = dot(perm, tok_ref[...], NN)
    cen = x - jnp.mean(x, -1, keepdims=True)
    inv = lax.rsqrt(jnp.mean(cen * cen, -1, keepdims=True) + EPS)
    std = cen * inv
    xhat[...] = std
    rstd[...] = inv
    gath[NORM, h] = (std * gain_ref[...]).astype(BF16)
    loads[1].wait()
    gath[COT, h] = dot(perm, cot_ref[...], NN).astype(BF16)
    pl.semaphore_wait(barrier, len(plane) + 2)

    def ag_copy(arr, way, t, blk):
        step = 1 - 2 * way
        return pltpu.make_async_remote_copy(
            src_ref=gath.at[arr, blk], dst_ref=gath.at[arr, blk],
            send_sem=ag_send.at[arr, way, t], recv_sem=ag_recv.at[arr, way, t],
            device_id={"head": h + step}, device_id_type=MESH,
        )

    def sends(way, t):
        if way == 0:
            return (h < n - 1) & (h >= t)
        return (h > 0) & (h < n - t)

    short = jnp.minimum(h, n - 1 - h)

    def arrival(k):
        paired = k <= 2 * short
        way = jnp.where(paired, lax.rem(k - 1, 2), jnp.where(2 * h > n - 1, 0, 1))
        t = jnp.where(paired, (k - 1) // 2, k - 1 - short)
        return way, t, 1 - 2 * way

    def arrived_block(k):
        way, t, step = arrival(k)
        return jnp.where(k == 0, h, h - step * (t + 1))

    def can_send(way):
        return jnp.where(way == 0, h < n - 1, h > 0)

    def receive(arr, k):
        way, t, step = arrival(k)
        blk = h - step * (t + 1)
        pltpu.make_async_remote_copy(
            src_ref=gath.at[arr, blk], dst_ref=gath.at[arr, blk],
            send_sem=ag_send.at[arr, way, t], recv_sem=ag_recv.at[arr, way, t],
            device_id={"head": h - step}, device_id_type=MESH,
        ).wait_recv()

        @pl.when(can_send(way))
        def _():
            ag_copy(arr, way, t + 1, blk).start()

        if arr == NORM:
            last = t + 1 == jnp.where(way == 0, h, n - 1 - h)

            @pl.when(last & can_send(way))
            def _():
                ag_copy(COT, way, 0, h).start()

    def in_copy(kind, k):
        tile = (tile_q, tile_g)[kind]
        if k == 0:
            src, dst, dev = tile.at[0, pl.ds(1, ucols - 1)], tile.at[n, pl.ds(1, ucols - 1)], at(-1, 0)
        elif k == n:
            src, dst, dev = tile.at[0, 0], tile.at[n, ucols], at(-1, -1)
        else:
            src, dst, dev = tile.at[k, 0], tile.at[k, ucols], at(0, -1)
        return pltpu.make_async_remote_copy(
            src_ref=src, dst_ref=dst, send_sem=in_send.at[kind, k], recv_sem=in_recv.at[kind, k],
            device_id=dev, device_id_type=MESH,
        )

    def project(kind, blk):
        if kind == 0:
            for s in range(3):
                out = dot(gath[NORM, blk], wq_ref[s], NN).astype(BF16)
                tile_q[blk, pl.ds(0, ucols), :, pl.ds(s * group, group)] = out.reshape(
                    ucols, UNIT, group
                )
        else:
            out = dot(gath[COT, blk], wp_ref[...], NT).astype(BF16)
            tile_g[blk, pl.ds(0, ucols)] = out.reshape(ucols, UNIT, group)
        for k in range(n):
            @pl.when(blk == k)
            def _():
                in_copy(kind, k).start()
                if k == 0:
                    in_copy(kind, n).start()

    for way in range(2):
        @pl.when(sends(way, 0))
        def _():
            ag_copy(NORM, way, 0, h).start()

        @pl.when(h == (0, n - 1)[way])
        def _():
            ag_copy(COT, way, 0, h).start()

    heads = group // HD
    span = 2 * WIN - 1
    chunk = onehot.shape[2]
    queries = chunk // (2 * HD)
    rows, ids = table_ref.shape

    @pl.loop(0, onehot.shape[0])
    def _(j):
        at_col = lax.broadcasted_iota(jnp.int32, (1, chunk), 1)
        q_at = j * queries + at_col // (2 * HD)
        k_at = at_col % HD
        qr, qc = window_place(q_at)
        kr, kc = window_place(k_at)
        index = (qr - kr + WIN - 1) * span + qc - kc + WIN - 1
        hot = lax.broadcasted_iota(jnp.int32, (ids, chunk), 0) == index
        onehot[j] = jnp.where(hot, 1.0, 0.0).astype(BF16)
        out = thirds(dot(parts_of(table_ref[...]), onehot[j], NN))
        for k in range(heads):
            for q in range(queries):
                bias[k, pl.ds(j * queries + q, 1), :] = out[k : k + 1, q * 2 * HD : (q + 1) * 2 * HD]

    loads[2].wait()
    loads[3].wait()

    @pl.loop(0, n)
    def _(k):
        @pl.when(k > 0)
        def _():
            receive(NORM, k)

        project(0, arrived_block(k))

    for k in range(n + 1):
        in_copy(0, k).wait_recv()

    lane = lax.broadcasted_iota(jnp.int32, (2 * WIN * WIN, 2 * HD), 1)
    first = lane < HD
    keep0 = jnp.where(first, 1.0, 0.0).astype(BF16)
    keep1 = jnp.where(first, 0.0, 1.0).astype(BF16)
    half = 2 * WIN * WIN
    scale = HD ** (-0.5)
    heads2 = group // (2 * HD)
    pairs2 = ucols // 4

    def places(i, jp):
        return [(2 * i + 1 + ur, 4 * jp + 1 + 2 * w) for w in range(2) for ur in range(2)]

    def load(tile, i, jp, at_lane):
        return jnp.concatenate(
            [
                tile[ur, pl.ds(uc, 2), :, pl.ds(at_lane, 2 * HD)].reshape(2 * UNIT, 2 * HD)
                for ur, uc in places(i, jp)
            ],
            0,
        )

    def save(tile, i, jp, at_lane, value):
        for k, (ur, uc) in enumerate(places(i, jp)):
            tile[ur, pl.ds(uc, 2), :, pl.ds(at_lane, 2 * HD)] = (
                value[2 * UNIT * k : 2 * UNIT * (k + 1)].astype(BF16).reshape(2, UNIT, 2 * HD)
            )

    def both(value):
        return jnp.concatenate([value * keep0, value * keep1], 0)

    def chosen(value):
        return jnp.where(first, value[:half], value[half:])

    def labels(i, jp, pos):
        window = pos // (WIN * WIN)
        prow, pcol = window_place(pos % (WIN * WIN))
        row = region((r * (n // 2) + i) * WIN + prow, nr * n * SHIFT)
        col = region(c * ncol + (2 * jp + window) * WIN + pcol, nc * ncol)
        return 16 * window + 3 * row + col

    def mask_of(i, jp):
        q_at = lax.broadcasted_iota(jnp.int32, (half, 1), 0)
        k_at = lax.broadcasted_iota(jnp.int32, (1, half), 1)
        same = labels(i, jp, q_at) == labels(i, jp, k_at)
        kept = (valid_ref[pl.ds(pairs2 * i + jp, 1), :] == 1) | (q_at == k_at)
        return jnp.where(same & kept, 0.0, -1e30)

    def forward(i, jp):
        m = mask_of(i, jp)
        for hp in range(heads2):
            base = hp * 2 * HD
            q, k, v = [load(tile_q, i, jp, base + s * group) for s in range(3)]
            b = [bias[2 * hp], bias[2 * hp], bias[2 * hp + 1], bias[2 * hp + 1]]
            s = dot(both(q), k, NT) * scale + jnp.concatenate(b, 0) + jnp.concatenate([m, m], 0)
            e = jnp.exp(s - jnp.max(s, -1, keepdims=True))
            p = e / jnp.sum(e, -1, keepdims=True)
            probs[pairs2 * i + jp, hp] = p
            save(back_a, i, jp, base, chosen(dot(p.astype(BF16), v, NN)))

    def backward(i, jp):
        for hp in range(heads2):
            base = hp * 2 * HD
            q, k, v = [load(tile_q, i, jp, base + s * group) for s in range(3)]
            dos = both(load(tile_g, i, jp, base))
            p = probs[pairs2 * i + jp, hp]
            dp = dot(dos, v, NT)
            save(back_d, i, jp, base + 2 * group, dot(p.astype(BF16), dos, TN))
            ds = p * (dp - jnp.sum(p * dp, -1, keepdims=True))
            dsb = ds.astype(BF16)
            save(back_d, i, jp, base, chosen(dot(dsb, k, NN) * scale))
            save(back_d, i, jp, base + group, dot(dsb, both(q), TN) * scale)
            tsum[hp] += ds

    def out_copy(kind, k):
        back = (back_a, back_d)[kind]
        if k == 0:
            src, dst, dev = back.at[n, pl.ds(1, ucols - 1)], back.at[0, pl.ds(1, ucols - 1)], at(1, 0)
        elif k == n:
            src, dst, dev = back.at[n, ucols], back.at[0, 0], at(1, 1)
        else:
            src, dst, dev = back.at[k, ucols], back.at[k, 0], at(0, 1)
        return pltpu.make_async_remote_copy(
            src_ref=src, dst_ref=dst, send_sem=out_send.at[kind, k], recv_sem=out_recv.at[kind, k],
            device_id=dev, device_id_type=MESH,
        )

    def windows(kind, step, between):
        @pl.loop(0, n // 2 * pairs2)
        def _(count):
            i = n // 2 - 1 - count // pairs2
            jp = pairs2 - 1 - lax.rem(count, pairs2)
            step(i, jp)
            for i_at in range(n // 2):
                @pl.when((i == i_at) & (jp == pairs2 - 1))
                def _():
                    out_copy(kind, 2 * i_at + 1).start()
                    out_copy(kind, 2 * i_at + 2).start()

            @pl.when((i == n // 2 - 1) & (jp == 0))
            def _():
                out_copy(kind, 0).start()

            between(count)

    def between_forward(count):
        @pl.when(count < n - 2)
        def _():
            receive(COT, count + 1)

    windows(0, forward, between_forward)
    for k in range(n + 1):
        out_copy(0, k).wait_recv()

    def block(back, d):
        return back[d, pl.ds(0, ucols)].reshape(part, back.shape[-1])

    def rs_copy(arr, way, d):
        step = 1 - 2 * way
        return pltpu.make_async_remote_copy(
            src_ref=terms.at[arr, d], dst_ref=recv.at[arr, way, d],
            send_sem=rs_send.at[arr, way, d], recv_sem=rs_recv.at[arr, way, d],
            device_id={"head": h + step}, device_id_type=MESH,
        )

    def rs_arrived(arr, way, d):
        step = 1 - 2 * way
        pltpu.make_async_remote_copy(
            src_ref=terms.at[arr, d], dst_ref=recv.at[arr, way, d],
            send_sem=rs_send.at[arr, way, d], recv_sem=rs_recv.at[arr, way, d],
            device_id={"head": h - step}, device_id_type=MESH,
        ).wait_recv()

    def order(k):
        far = n - 1 - k // 2
        near = k // 2
        return jnp.where((lax.rem(k, 2) == 0) == (2 * h < n - 1), far, near)

    def rs_start(arr):
        @pl.loop(0, n)
        def _(k):
            d = order(k)
            if arr == 0:
                term = dot(block(back_a, d), wp_ref[...], NN)
            else:
                grads = block(back_d, d)
                term = sum(
                    dot(grads[:, s * group : (s + 1) * group], wq_ref[s], NT) for s in range(3)
                )
            terms[arr, d] = term.astype(BF16)

            @pl.when((h == 0) & (d > 0))
            def _():
                rs_copy(arr, 0, d).start()

            @pl.when((h == n - 1) & (d < n - 1))
            def _():
                rs_copy(arr, 1, d).start()

    def rs_transit(arr, k):
        d = order(k)

        @pl.when(((h < d) & (h > 0)) | ((h > d) & (h < n - 1)))
        def _():
            way = jnp.where(h < d, 0, 1)
            rs_arrived(arr, way, d)
            terms[arr, d] = (terms[arr, d].astype(F32) + recv[arr, way, d].astype(F32)).astype(BF16)
            rs_copy(arr, way, d).start()

    def total(arr):
        sides = [h > 0, h < n - 1]
        for way in range(2):
            @pl.when(sides[way])
            def _():
                rs_arrived(arr, way, h)

            @pl.when(jnp.logical_not(sides[way]))
            def _():
                recv[arr, way, h] = jnp.zeros((part, width), BF16)
        return (
            terms[arr, h].astype(F32) + recv[arr, 0, h].astype(F32) + recv[arr, 1, h].astype(F32)
        )

    rs_start(0)

    @pl.loop(0, n)
    def _(k):
        @pl.when(k == n - 1)
        def _():
            receive(COT, k)

        project(1, arrived_block(k))

    for k in range(n + 1):
        in_copy(1, k).wait_recv()

    tsum[...] = jnp.zeros_like(tsum)
    def between_backward(count):
        @pl.when(count > 0)
        def _():
            rs_transit(0, count - 1)

    windows(1, backward, between_backward)

    for k in range(n + 1):
        out_copy(1, k).wait_recv()
    rs_start(1)

    def pl_copy(kind, o):
        dr, dc = plane[o]
        there = at(dr, dc)
        if kind == 0:
            src, dst = wsend.at[there["row"] * nc + there["col"]], wrecv.at[o]
        else:
            src, dst = tsend, trecv.at[o]
        return pltpu.make_async_remote_copy(
            src_ref=src, dst_ref=dst, send_sem=pl_send.at[kind, o], recv_sem=pl_recv.at[kind, o],
            device_id=there, device_id_type=MESH,
        )

    wide = 2 * 128

    @pl.loop(0, width // wide)
    def _(j):
        attn = back_a[pl.ds(0, n), pl.ds(0, ucols)].reshape(n * part, group)
        cols = pl.ds(pl.multiple_of(j * wide, wide), wide)
        wterm = dot(attn, gath[COT, :, :, cols].reshape(n * part, wide), TN)
        if direct:
            piece = width // (nr * nc)
            for k in range(wide // piece):
                wsend[wide // piece * j + k] = wterm[:, k * piece : (k + 1) * piece].astype(BF16)
        else:
            pg_ref[:, cols] = wterm

    if direct:
        for o in range(len(plane)):
            pl_copy(0, o).start()
    rs_transit(1, 0)

    for k in range(heads):
        hp, at_row = k // 2, k % 2 * half
        bias[k] = tsum[hp, at_row : at_row + HD] + tsum[hp, at_row + HD : at_row + half]
    flat[...] = jnp.zeros_like(flat)
    tsend[...] = jnp.zeros_like(tsend)

    @pl.loop(0, onehot.shape[0])
    def _(j):
        for k in range(heads):
            for q in range(queries):
                flat[k : k + 1, q * 2 * HD : (q + 1) * 2 * HD] = bias[k, pl.ds(j * queries + q, 1), :]
        tsend[...] += thirds(dot(parts_of(flat[...]), onehot[j], NT))

    if direct:
        for o in range(len(plane)):
            pl_copy(1, o).start()
    else:
        ts_ref[...] = tsend[...]

    @pl.loop(1, n - 1)
    def _(k):
        rs_transit(1, k)

    mixed = dot(perm, tok_ref[...], NN) + total(0)
    mixed_ref[...] = dot(perm, mixed.astype(BF16), TN).astype(BF16)

    if direct:
        for o in range(len(plane)):
            for kind in range(2):
                pl_copy(kind, o).wait_recv()
        wsum = wsend[r * nc + c].astype(F32)
        tall = tsend[...]
        for o in range(len(plane)):
            wsum = wsum + wrecv[o].astype(F32)
            tall = tall + trecv[o]
        pg_ref[...] = wsum * pg_scale
        ts_ref[...] = tall
        for o in range(len(plane)):
            for kind in range(2):
                pl_copy(kind, o).wait_send()

    gg = total(1) * gain_ref[...]
    std = xhat[...]
    tg = gath[COT, h].astype(F32) + rstd[...] * (
        gg - jnp.mean(gg, -1, keepdims=True) - std * jnp.mean(gg * std, -1, keepdims=True)
    )
    tg_ref[...] = dot(perm, tg.astype(BF16), TN).astype(BF16)

    for arr in range(2):
        for way in range(2):
            for t in range(n - 1):
                @pl.when(sends(way, t))
                def _():
                    ag_copy(arr, way, t, h - (1 - 2 * way) * t).wait_send()
    for kind in range(2):
        for k in range(n + 1):
            in_copy(kind, k).wait_send()
            out_copy(kind, k).wait_send()
    for arr in range(2):
        for d in range(n):
            if d > 0:
                @pl.when(h < d)
                def _():
                    rs_copy(arr, 0, d).wait_send()
            if d < n - 1:
                @pl.when(h > d)
                def _():
                    rs_copy(arr, 1, d).wait_send()


def on_device(n, nr, nc, tokens, valid, gain, w_qkv, w_proj, rel_table, cotangent):
    part_rows, ncol, width = tokens.shape
    tile_rows = part_rows * n
    part = part_rows * ncol
    heads = rel_table.shape[1]
    group = heads * HD
    pairs = heads // 2
    pos = WIN * WIN
    ucols = ncol // SHIFT

    def to_pairs(block):
        block = block.reshape(tile_rows // WIN, 2, SHIFT, ncol // WIN, 2, SHIFT)
        return block.transpose(0, 3, 1, 4, 2, 5).reshape(-1, 2 * pos)

    rows, ids = -(-heads // 16) * 16, 256
    table = jnp.pad(rel_table.T, ((0, rows - heads), (0, ids - rel_table.shape[0])))
    scale = 1.0 / math.sqrt(tile_rows * ncol * nr * nc)
    direct = nr * nc <= 8
    if direct:
        plane = [(dr, dc) for dr in range(nr) for dc in range(nc) if (dr, dc) != (0, 0)]
    else:
        six = [(1, 0), (nr - 1, 0), (0, 1), (0, nc - 1), (1, 1), (nr - 1, nc - 1)]
        plane = sorted(set(six))
    count = len(plane)
    piece = width // (nr * nc)
    vmem = pl.BlockSpec(memory_space=pltpu.VMEM)
    hbm = pl.BlockSpec(memory_space=pltpu.HBM)
    dma = pltpu.SemaphoreType.DMA
    mixed, token_gradient, wsum, tall = pl.pallas_call(
        functools.partial(kernel, (n, nr, nc, tuple(plane), direct, ncol, scale)),
        out_shape=(
            jax.ShapeDtypeStruct((part, width), BF16),
            jax.ShapeDtypeStruct((part, width), BF16),
            jax.ShapeDtypeStruct((group, piece if direct else width), F32),
            jax.ShapeDtypeStruct((rows, ids), F32),
        ),
        in_specs=[hbm, hbm, vmem, hbm, hbm, vmem, vmem],
        out_specs=[vmem] * 4,
        scratch_shapes=[
            pltpu.VMEM((part, width), F32),
            pltpu.VMEM((part, 1), F32),
            pltpu.VMEM((2, n, part, width), BF16),
            pltpu.VMEM((n + 1, ucols + 1, UNIT, 3 * group), BF16),
            pltpu.VMEM((n + 1, ucols + 1, UNIT, group), BF16),
            pltpu.VMEM((n + 1, ucols + 1, UNIT, group), BF16),
            pltpu.VMEM((n + 1, ucols + 1, UNIT, 3 * group), BF16),
            pltpu.VMEM((n * ucols // 8, pairs, 4 * pos, 2 * pos), F32),
            pltpu.VMEM((2, n, part, width), BF16),
            pltpu.VMEM((2, 2, n, part, width), BF16),
            pltpu.VMEM((nr * nc, group, piece) if direct else (1, 16, 128), BF16),
            pltpu.VMEM((count, group, piece) if direct else (1, 16, 128), BF16),
            pltpu.VMEM((rows, ids), F32),
            pltpu.VMEM((count, rows, ids) if direct else (1, 16, 128), F32),
            pltpu.VMEM((pairs, 4 * pos, 2 * pos), F32),
            pltpu.VMEM((pos // 4, ids, 8 * HD), BF16),
            pltpu.VMEM((heads, pos, 2 * HD), F32),
            pltpu.VMEM((rows, 8 * HD), F32),
            pltpu.VMEM((part, width), BF16),
            pltpu.VMEM((part, width), BF16),
            pltpu.VMEM((3, width, group), BF16),
            pltpu.VMEM((group, width), BF16),
            dma((4,)),
            dma((2, 2, n)),
            dma((2, 2, n)),
            dma((2, n + 1)),
            dma((2, n + 1)),
            dma((2, n + 1)),
            dma((2, n + 1)),
            dma((2, 2, n)),
            dma((2, 2, n)),
            dma((2, count)),
            dma((2, count)),
        ],
        compiler_params=pltpu.CompilerParams(
            collective_id=0, has_side_effects=True, vmem_limit_bytes=53 * 1024 * 1024
        ),
    )(
        tokens.reshape(part, width),
        cotangent.reshape(part, width),
        gain[None],
        w_qkv.transpose(1, 0, 2),
        w_proj,
        table,
        to_pairs(valid),
    )
    if not direct:
        wsum = lax.psum_scatter(wsum, ("row", "col"), scatter_dimension=1, tiled=True) * scale
        tall = lax.psum(tall, ("row", "col"))
    table_grad = tall[:heads, : rel_table.shape[0]].T * (WIN * scale)
    return (
        mixed.reshape(part_rows, ncol, width),
        token_gradient.reshape(part_rows, ncol, width),
        wsum,
        table_grad,
    )


def solution(mesh):
    n, nr, nc = (mesh.shape[name] for name in ("head", "row", "col"))
    return jax.shard_map(
        functools.partial(on_device, n, nr, nc),
        mesh=mesh,
        in_specs=(
            P(("row", "head"), "col", None),
            P("row", "col"),
            P(),
            P(None, None, "head"),
            P("head", None),
            P(None, "head"),
            P(("row", "head"), "col", None),
        ),
        out_specs=(
            P(("row", "head"), "col", None),
            P(("row", "head"), "col", None),
            P("head", ("row", "col")),
            P(None, "head"),
        ),
        check_vma=False,
    )
```
